32 devices in a mesh: batch: 4 (over x, core), seq: 8 (over z, y).
Axes of the slice: x: 2, y: 2, z: 4, core: 2. Of those that a mesh axis runs over, the one named last changes fastest.
Arguments:
- token_ids: int32 [4, 1024], P('batch', 'seq'), may hold values from 0 to 32127
- embedding: bfloat16 [32128, 768], P(('batch', 'seq')), may hold values from -6 to 6
- gain_attn: bfloat16 [2, 768], P(None, ('batch', 'seq')), may hold values from 0.5 to 1.5
- w_qkv: bfloat16 [2, 768, 2304], P(None, ('batch', 'seq')), may hold values from -0.21875 to 0.21875
- w_proj: bfloat16 [2, 768, 768], P(None, ('batch', 'seq')), may hold values from -1.75 to 1.75
- gain_ffn: bfloat16 [2, 768], P(None, ('batch', 'seq')), may hold values from 0.5 to 1.5
- w_in: bfloat16 [2, 768, 3072], P(None, ('batch', 'seq')), may hold values from -0.21875 to 0.21875
- w_back: bfloat16 [2, 3072, 768], P(None, ('batch', 'seq')), may hold values from -0.109375 to 0.109375
- mix_pre: float32 [2, 12, 12], replicated, may hold values from -2.5 to 2.5
- mix_post: float32 [2, 12, 12], replicated, may hold values from -2.5 to 2.5
- cotangent: bfloat16 [4, 1024, 768], P('batch', 'seq'), may hold values from -6 to 6
Outputs:
- output: bfloat16 [4, 1024, 768], P('batch', 'seq')
- embedding_grad: float32 [32128, 768], P(('batch', 'seq'))
- gain_attn_grad: float32 [2, 768], P(None, ('batch', 'seq'))
- w_qkv_grad: float32 [2, 768, 2304], P(None, ('batch', 'seq'))
- w_proj_grad: float32 [2, 768, 768], P(None, ('batch', 'seq'))
- gain_ffn_grad: float32 [2, 768], P(None, ('batch', 'seq'))
- w_in_grad: float32 [2, 768, 3072], P(None, ('batch', 'seq'))
- w_back_grad: float32 [2, 3072, 768], P(None, ('batch', 'seq'))
- mix_pre_grad: float32 [2, 12, 12], replicated
- mix_post_grad: float32 [2, 12, 12], replicated
The draws below stay inside these ranges and needn't reach their ends.
Inputs may be any that keep to these rules, and one draw needn't show every extreme that they name: `token_ids`: each id names a row of the embedding table.
All inputs are finite; a program needn't handle non-finite values.
Results may differ from the reference program's by a relative error of at most 0.04.
Values may be sent and summed in bfloat16 or wider, within the bound.
No kernel may reach another device: no remote copies, remote signals or barrier semaphores. Data moves between devices by JAX's collectives and lax.ppermute only.
A program may use at most 256 MiB of HBM per device.

```python
import math
import jax
import jax.numpy as jnp
import numpy as np
from jax import lax

D = 768
H = 12
E = 64
FF = 3072
V = 32128
LAYERS = 2
LENGTH = 1024
SEQS = 4


def place_ends(drawn, own_key, least, high):
    longest = drawn.shape.index(max(drawn.shape))
    spots = []
    for shift in (0, 1):
        where = [jax.random.randint(jax.random.fold_in(own_key, axis), (), 0, length) for axis, length in enumerate(drawn.shape)]
        where[longest] = (where[longest] + shift) % drawn.shape[longest]
        spots.append(tuple(where))
    return drawn.at[spots[0]].set(least).at[spots[1]].set(high)


def levels(key, shape, split, low, largest):
    def one(dim, blocks):
        steps = jax.random.uniform(jax.random.fold_in(jax.random.fold_in(key, 6), dim), (blocks,), jnp.float32, low / len(split), largest / len(split))
        return jnp.repeat(jnp.exp(steps), shape[dim] // blocks).reshape((-1,) + (1,) * (len(shape) - dim - 1))

    level = one(*split[0])
    for cut in split[1:]:
        level = level * one(*cut)
    return level


def rank_bounds(count, lean):
    loads = [(1 << 20) // math.isqrt(grade ** lean) + 1 for grade in range(1, count + 1)]
    spread = 1 + sum(loads) // (1 << 30)
    return np.cumsum(np.array([max(1, weight // spread) for weight in loads]))


def ranked_ids(rng, extent, count, slope):
    listing = rank_bounds(count, slope)
    ticket = jax.random.randint(jax.random.fold_in(rng, 1), extent, 0, int(listing[count - 1]))
    standing = jnp.searchsorted(jnp.asarray(listing, jnp.int32), ticket, side="right")
    return jax.random.permutation(jax.random.fold_in(rng, 2), count)[standing].astype(jnp.int32)


def noise(rng, dims, width, most, pieces=(), kind=jnp.bfloat16):
    level = levels(rng, dims, pieces, -0.22, 0.18) if pieces else 1.0
    drawn = jax.random.normal(rng, dims, jnp.float32) * width * level
    return jnp.minimum(jnp.maximum(drawn, -most), most).astype(kind)


def setup_inputs(seed: int = 0) -> dict:
    keys = jax.random.split(jax.random.key(seed), 12)
    token_ids = place_ends(ranked_ids(keys[0], (SEQS, LENGTH), V, 2), jax.random.fold_in(keys[0], 3), 0, V - 1).astype(jnp.int32)
    embedding = noise(keys[1], (V, D), 1.0, 6.0, ((0, 32),))
    gain_attn = jnp.clip(1.0 + 0.1 * jax.random.normal(keys[2], (LAYERS, D), jnp.float32), 0.5, 1.5).astype(jnp.bfloat16)
    w_qkv = noise(keys[3], (LAYERS, D, 3 * D), D ** -0.5, 0.21875, ((1, 32),))
    w_proj = noise(keys[4], (LAYERS, D, D), (max(1, D * 16 // LENGTH)) ** -0.5, 1.75, ((1, 32),))
    gain_ffn = jnp.clip(1.0 + 0.1 * jax.random.normal(keys[5], (LAYERS, D), jnp.float32), 0.5, 1.5).astype(jnp.bfloat16)
    w_in = noise(keys[6], (LAYERS, D, FF), D ** -0.5, 0.21875, ((1, 32),))
    w_back = noise(keys[7], (LAYERS, FF, D), FF ** -0.5, 0.109375, ((1, 32),))
    mix_pre = noise(keys[8], (LAYERS, H, H), 0.45, 2.5, (), jnp.float32)
    mix_post = noise(keys[9], (LAYERS, H, H), 0.45, 2.5, (), jnp.float32)
    cotangent = noise(keys[10], (SEQS, LENGTH, D), 1.0, 6.0, ((0, 4), (1, 8)))
    return {"token_ids": token_ids, "embedding": embedding, "gain_attn": gain_attn, "w_qkv": w_qkv, "w_proj": w_proj, "gain_ffn": gain_ffn, "w_in": w_in, "w_back": w_back, "mix_pre": mix_pre, "mix_post": mix_post, "cotangent": cotangent}


@jax.custom_vjp
def low(v):
    return lax.optimization_barrier(v.astype(jnp.bfloat16)).astype(jnp.float32)

@jax.custom_vjp
def low_back(v):
    return v

def low_keep(v):
    return (low(v), None)

def low_pass(kept, grad):
    return (grad,)

def back_keep(v):
    return (v, None)

def back_low(kept, grad):
    return (low(grad),)
low.defvjp(low_keep, low_pass)
low_back.defvjp(back_keep, back_low)
HIGHEST = lax.Precision.HIGHEST

def rms_norm(values, gain):
    return values * lax.rsqrt(lax.optimization_barrier(jnp.mean(values * values, axis=-1, keepdims=True)) + 1e-06) * gain

def matmul(left, right):
    return jnp.dot(left, right, precision=HIGHEST)

def attention(queries, keys_all, values_all, mixing_pre, mixing_post):
    length = queries.shape[0]
    block_rows = min(512, length)
    block_count = length // block_rows
    key_heads = keys_all.reshape(length, H, E)
    value_heads = values_all.reshape(length, H, E)
    query_blocks = queries.reshape(block_count, block_rows, H, E)
    key_pos = jnp.arange(length, dtype=jnp.int32)

    def one_block(inputs):
        query_block, block_index = inputs
        query_pos = block_index * block_rows + jnp.arange(block_rows, dtype=jnp.int32)
        scores = jnp.einsum('thd,khd->htk', query_block, key_heads, precision=HIGHEST) * E ** (-0.5)
        scores = low_back(scores)
        logits = jnp.einsum('htk,hg->gtk', scores, mixing_pre, precision=HIGHEST)
        allowed = key_pos[None, :] <= query_pos[:, None]
        logits = jnp.where(allowed[None], logits, -1e+30)
        normalized = jax.nn.softmax(logits, axis=-1)
        mixture = low(jnp.einsum('gtk,gf->ftk', normalized, mixing_post, precision=HIGHEST))
        return jnp.einsum('ftk,kfd->tfd', mixture, value_heads, precision=HIGHEST)
    outputs = lax.map(jax.checkpoint(one_block), (query_blocks, jnp.arange(block_count, dtype=jnp.int32)))
    return outputs.reshape(length, D)

def forward(params, token_row):
    embed_table, attn_gain, qkv_weight, proj_weight, ffn_gain, in_weight, back_weight, mixing_pre, mixing_post = params
    stream = low_back(embed_table[token_row])
    for layer_index in range(LAYERS):
        normed = low(rms_norm(stream, attn_gain[layer_index]))
        projected = matmul(normed, qkv_weight[layer_index])
        queries = low_back(low(projected[:, :D]))
        keys_all = low_back(low(projected[:, D:2 * D]))
        values_all = low_back(low(projected[:, 2 * D:]))
        attended = attention(queries, keys_all, values_all, mixing_pre[layer_index], mixing_post[layer_index])
        attended = low_back(low(attended))
        stream = stream + low_back(matmul(attended, proj_weight[layer_index]))
        normed_ffn = low(rms_norm(stream, ffn_gain[layer_index]))
        hidden_pre = low_back(matmul(normed_ffn, in_weight[layer_index]))
        activated = low(jax.nn.gelu(hidden_pre, approximate=True))
        stream = stream + low_back(matmul(activated, back_weight[layer_index]))
    return stream

def reference(token_ids, embedding, gain_attn, w_qkv, w_proj, gain_ffn, w_in, w_back, mix_pre, mix_post, cotangent):
    params = (embedding.astype(jnp.float32), gain_attn.astype(jnp.float32), w_qkv.astype(jnp.float32), w_proj.astype(jnp.float32), gain_ffn.astype(jnp.float32), w_in.astype(jnp.float32), w_back.astype(jnp.float32), mix_pre.astype(jnp.float32), mix_post.astype(jnp.float32))

    def per_sequence(totals, inputs):
        token_row, output_grad = inputs
        result, pullback = jax.vjp(lambda *weights: forward(weights, token_row), *params)
        gradients = pullback(output_grad.astype(jnp.float32))
        totals = jax.tree.map(lambda total_part, new_part: total_part + new_part, totals, tuple(gradients))
        return (totals, result.astype(jnp.bfloat16))
    initial = jax.tree.map(jnp.zeros_like, params)
    totals, outputs = lax.scan(per_sequence, initial, (token_ids, cotangent))
    return (outputs, totals[0], totals[1], totals[2], totals[3], totals[4], totals[5], totals[6], totals[7], totals[8])
```

```python
import functools

import jax
import jax.numpy as jnp
from jax import lax
from jax.experimental import pallas as pl
from jax.experimental.pallas import tpu as pltpu
from jax.sharding import PartitionSpec as P

D = 768
H = 12
E = 64
LAYERS = 2
AXES = ("batch", "seq")
NEGATIVE = -1e30
CHUNK = 256
F32 = jnp.float32
BF16 = jnp.bfloat16


class Geometry:
    def __init__(self, mesh):
        self.b = mesh.shape["batch"]
        self.n = mesh.shape["seq"]
        self.r = self.n // self.b
        self.count = self.b * self.n
        self.core = self.n
        low = list(range(self.r))
        high = [k * self.n for k in range(0, self.b, 2)]
        self.plane = [h + l for h in high for l in low]
        self.zs = [k * self.r for k in range(self.b)]
        self.order = [c + p + z for c in (0, self.core) for p in self.plane for z in self.zs]

    def rank_mask(self, mask):
        return (mask // self.n) * self.r + mask % self.n

    def device(self, sequence, rank):
        return (rank // self.r) * self.n + sequence * self.r + rank % self.r


def swap(value, mask, count):
    return lax.ppermute(value, AXES, [(p, p ^ mask) for p in range(count)])


def dot(a, b, contract):
    return lax.dot_general(a, b, (contract, ((), ())), preferred_element_type=F32)


def load_keys(masks, half, rank, pieces, kv, sems):
    n = len(masks)
    copies = []
    for index, mask in enumerate(masks):
        owner = rank ^ mask
        for part, place in ((0, owner), (1, 2 * n - 1 - owner)):
            start = pl.multiple_of(place * half, half)
            copies.append(
                pltpu.make_async_copy(
                    pieces[index].at[pl.ds(part * half, half)],
                    kv.at[pl.ds(start, half)],
                    sems.at[2 * index + part],
                )
            )
    for copy in copies:
        copy.start()
    return copies


def mixed_rows(rows, weights):
    return jnp.concatenate([rows * weights[g : g + 1, :] for g in range(H)], axis=0)


def forward_kernel(masks, half, rank_ref, q_ref, pre_ref, post_ref, *rest):
    n = len(masks)
    pieces = rest[:n]
    o_ref, lse_ref, pv_ref = rest[n : n + 3]
    kv, qg, logits, top, total, acc, sems = rest[n + 3 :]
    rank = rank_ref[0]
    rows = H * half
    copies = load_keys(masks, half, rank, pieces, kv, sems)
    for copy in copies:
        copy.wait()
    for part in range(2):
        place = rank if part == 0 else 2 * n - 1 - rank
        live = (place * half + half + CHUNK - 1) // CHUNK
        q_part = q_ref[part * half : (part + 1) * half, :].astype(F32)
        qg[...] = mixed_rows(q_part, pre_ref[...]).astype(BF16)
        top[...] = jnp.full((rows, 128), NEGATIVE, F32)
        total[...] = jnp.zeros((rows, 128), F32)
        acc[...] = jnp.zeros((rows, D), F32)
        spot = place * half + lax.broadcasted_iota(jnp.int32, (rows, CHUNK), 0) % half
        lane = lax.broadcasted_iota(jnp.int32, (rows, CHUNK), 1)

        def score(c, carry):
            start = pl.multiple_of(c * CHUNK, CHUNK)
            found = dot(qg[...], kv[pl.ds(start, CHUNK), :D], ((1,), (1,)))
            found = jnp.where(start + lane <= spot, found, NEGATIVE)
            logits[c] = found
            best = found[:, :128]
            for k in range(1, CHUNK // 128):
                best = jnp.maximum(best, found[:, k * 128 : (k + 1) * 128])
            top[...] = jnp.maximum(top[...], best)
            return carry

        lax.fori_loop(0, live, score, 0)
        row_max = jnp.max(top[...], axis=1, keepdims=True)

        def weigh(c, carry):
            start = pl.multiple_of(c * CHUNK, CHUNK)
            prob = jnp.exp(logits[c] - row_max)
            part_sum = prob[:, :128]
            for k in range(1, CHUNK // 128):
                part_sum = part_sum + prob[:, k * 128 : (k + 1) * 128]
            total[...] += part_sum
            acc[...] += dot(prob.astype(BF16), kv[pl.ds(start, CHUNK), D:], ((1,), (0,)))
            return carry

        lax.fori_loop(0, live, weigh, 0)
        row_sum = jnp.sum(total[...], axis=1, keepdims=True)
        scale = 1.0 / row_sum
        lse = jnp.broadcast_to(row_max + jnp.log(row_sum), (rows, 128))
        lse_ref[part] = jnp.transpose(lse)[:8, :]
        out = jnp.zeros((half, D), F32)
        for g in range(H):
            normal = acc[g * half : (g + 1) * half, :] * scale[g * half : (g + 1) * half, :]
            pv_ref[part, g * half : (g + 1) * half, :] = normal.astype(BF16)
            out = out + normal * post_ref[g : g + 1, :]
        o_ref[part * half : (part + 1) * half, :] = out.astype(BF16)


def backward_kernel(masks, half, rank_ref, q_ref, go_ref, lse_ref, pv_ref, pre_ref, post_ref, *rest):
    n = len(masks)
    pieces = rest[:n]
    gq_ref, pre_grad_ref, post_grad_ref = rest[n : n + 3]
    grads = rest[n + 3 : 2 * n + 3]
    kv, qg, gg, gk, gv, acc, sems, out_sems = rest[2 * n + 3 :]
    rank = rank_ref[0]
    rows = H * half
    copies = load_keys(masks, half, rank, pieces, kv, sems)
    gk[...] = jnp.zeros(gk.shape, F32)
    gv[...] = jnp.zeros(gv.shape, F32)
    pre_grad_ref[...] = jnp.zeros(pre_grad_ref.shape, F32)
    post_grad_ref[...] = jnp.zeros(post_grad_ref.shape, F32)
    for copy in copies:
        copy.wait()
    for part in range(2):
        place = rank if part == 0 else 2 * n - 1 - rank
        live = (place * half + half + CHUNK - 1) // CHUNK
        q_part = q_ref[part * half : (part + 1) * half, :].astype(F32)
        go_part = go_ref[part * half : (part + 1) * half, :].astype(F32)
        row_dots = []
        for g in range(H):
            qg[g * half : (g + 1) * half, :] = (q_part * pre_ref[g : g + 1, :]).astype(BF16)
            mixed = go_part * post_ref[g : g + 1, :]
            gg[g * half : (g + 1) * half, :] = mixed.astype(BF16)
            normal = pv_ref[part, g * half : (g + 1) * half, :].astype(F32)
            row_dots.append(jnp.sum(mixed * normal, axis=1, keepdims=True))
            post_grad_ref[g : g + 1, :] += jnp.sum(go_part * normal, axis=0, keepdims=True)
        row_dot = jnp.broadcast_to(jnp.concatenate(row_dots, axis=0), (rows, 128))
        row_dot = jnp.transpose(row_dot)[:1, :]
        lse = lse_ref[part][:1, :]
        acc[...] = jnp.zeros((rows, D), F32)
        spot = place * half + lax.broadcasted_iota(jnp.int32, (CHUNK, rows), 1) % half
        line = lax.broadcasted_iota(jnp.int32, (CHUNK, rows), 0)

        def block(c, carry):
            start = pl.multiple_of(c * CHUNK, CHUNK)
            keys = kv[pl.ds(start, CHUNK), :D]
            values = kv[pl.ds(start, CHUNK), D:]
            found = dot(keys, qg[...], ((1,), (1,)))
            found = jnp.where(start + line <= spot, found, NEGATIVE)
            prob = jnp.exp(found - lse)
            grad_prob = dot(values, gg[...], ((1,), (1,)))
            grad_logit = (prob * (grad_prob - row_dot)).astype(BF16)
            gv[pl.ds(start, CHUNK), :] += dot(prob.astype(BF16), gg[...], ((1,), (0,)))
            gk[pl.ds(start, CHUNK), :] += dot(grad_logit, qg[...], ((1,), (0,)))
            acc[...] += dot(grad_logit, keys, ((0,), (0,)))
            return carry

        lax.fori_loop(0, live, block, 0)
        gq = jnp.zeros((half, D), F32)
        for g in range(H):
            found = acc[g * half : (g + 1) * half, :]
            gq = gq + found * pre_ref[g : g + 1, :]
            pre_grad_ref[g : g + 1, :] += jnp.sum(found * q_part, axis=0, keepdims=True)
        gq_ref[part * half : (part + 1) * half, :] = gq.astype(BF16)
    kv[:, :D] = gk[...].astype(BF16)
    kv[:, D:] = gv[...].astype(BF16)
    copies = []
    for index, mask in enumerate(masks):
        owner = rank ^ mask
        for part, place in ((0, owner), (1, 2 * n - 1 - owner)):
            start = pl.multiple_of(place * half, half)
            copies.append(
                pltpu.make_async_copy(
                    kv.at[pl.ds(start, half)],
                    grads[index].at[pl.ds(part * half, half)],
                    out_sems.at[2 * index + part],
                )
            )
    for copy in copies:
        copy.start()
    for copy in copies:
        copy.wait()


VMEM = pl.BlockSpec(memory_space=pltpu.VMEM)
SMEM = pl.BlockSpec(memory_space=pltpu.SMEM)
ANY = pl.BlockSpec(memory_space=pl.ANY)
LIMIT = pltpu.CompilerParams(vmem_limit_bytes=58 * 2**20)


def attend(masks, rank, queries, pieces, pre, post):
    n = len(masks)
    tokens = queries.shape[0]
    half = tokens // 2
    rows = H * half
    length = n * tokens
    return pl.pallas_call(
        functools.partial(forward_kernel, masks, half),
        out_shape=(
            jax.ShapeDtypeStruct((tokens, D), BF16),
            jax.ShapeDtypeStruct((2, 8, rows), F32),
            jax.ShapeDtypeStruct((2, rows, D), BF16),
        ),
        in_specs=[SMEM, VMEM, VMEM, VMEM] + [ANY] * n,
        out_specs=(VMEM, VMEM, VMEM),
        scratch_shapes=[
            pltpu.VMEM((length, 2 * D), BF16),
            pltpu.VMEM((rows, D), BF16),
            pltpu.VMEM((length // CHUNK, rows, CHUNK), F32),
            pltpu.VMEM((rows, 128), F32),
            pltpu.VMEM((rows, 128), F32),
            pltpu.VMEM((rows, D), F32),
            pltpu.SemaphoreType.DMA((2 * n,)),
        ],
        compiler_params=LIMIT,
        name="attend",
    )(rank, queries, pre, post, *pieces)


def attend_back(masks, rank, queries, grad_out, lse, pv, pieces, pre, post):
    n = len(masks)
    tokens = queries.shape[0]
    half = tokens // 2
    rows = H * half
    length = n * tokens
    outs = pl.pallas_call(
        functools.partial(backward_kernel, masks, half),
        out_shape=(
            jax.ShapeDtypeStruct((tokens, D), BF16),
            jax.ShapeDtypeStruct((H, D), F32),
            jax.ShapeDtypeStruct((H, D), F32),
        )
        + tuple(jax.ShapeDtypeStruct((tokens, 2 * D), BF16) for _ in masks),
        in_specs=[SMEM] + [VMEM] * 6 + [ANY] * n,
        out_specs=(VMEM, VMEM, VMEM) + (ANY,) * n,
        scratch_shapes=[
            pltpu.VMEM((length, 2 * D), BF16),
            pltpu.VMEM((rows, D), BF16),
            pltpu.VMEM((rows, D), BF16),
            pltpu.VMEM((length, D), F32),
            pltpu.VMEM((length, D), F32),
            pltpu.VMEM((rows, D), F32),
            pltpu.SemaphoreType.DMA((2 * n,)),
            pltpu.SemaphoreType.DMA((2 * n,)),
        ],
        compiler_params=LIMIT,
        name="attend_back",
    )(rank, queries, grad_out, lse, pv, pre, post, *pieces)
    return outs[0], outs[1], outs[2], outs[3:]


def mm(a, b):
    return jnp.dot(a, b, preferred_element_type=F32)


def mm_t(a, b):
    return lax.dot_general(a, b, (((1,), (1,)), ((), ())), preferred_element_type=F32)


def t_mm(a, b):
    return lax.dot_general(a, b, (((0,), (0,)), ((), ())), preferred_element_type=F32)


def norm_parts(x):
    return lax.rsqrt(jnp.mean(x * x, axis=-1, keepdims=True) + 1e-06)


def norm_back(x, gain, grad):
    r = norm_parts(x)
    gain_grad = jnp.sum(grad * x * r, axis=0)
    scaled = grad * gain
    x_grad = r * scaled - x * (r * r * r) * jnp.mean(scaled * x, axis=-1, keepdims=True)
    return x_grad, gain_grad


def shards(
    geo,
    token_ids,
    embedding,
    gain_attn,
    w_qkv,
    w_proj,
    gain_ffn,
    w_in,
    w_back,
    mix_pre,
    mix_post,
    cotangent,
):
    n, r, count, core = geo.n, geo.r, geo.count, geo.core
    tokens = token_ids.size
    half = tokens // 2
    i = lax.axis_index("batch")
    j = lax.axis_index("seq")
    me = i * n + j
    rank = i * r + j % r
    rank_arg = rank.reshape(1).astype(jnp.int32)
    share = w_qkv.shape[1]
    back_share = w_back.shape[1]
    folds = back_share // share
    ff = w_in.shape[2]
    sw = functools.partial(swap, count=count)

    columns = []
    for l in range(LAYERS):
        inward = w_in[l].reshape(share, count, folds, share).transpose(0, 2, 1, 3).reshape(share, ff)
        outward = w_back[l].reshape(folds, share, D).transpose(1, 0, 2).reshape(share, folds * D)
        columns += [w_qkv[l], w_proj[l], inward, outward]
    gains = jnp.stack([gain_attn[0], gain_ffn[0], gain_attn[1], gain_ffn[1]], axis=1)
    columns.append(jnp.pad(gains, ((0, 0), (0, 124))))
    weights = lax.all_gather(jnp.concatenate(columns, axis=1), AXES, axis=0, tiled=True)
    width = 4 * D + 2 * ff

    def layer_weights(l):
        w = weights[:, l * width : (l + 1) * width]
        outward = w[:, 4 * D + ff :].reshape(D, folds, D).transpose(1, 0, 2).reshape(ff, D)
        gain = weights[:, LAYERS * width + 2 * l : LAYERS * width + 2 * l + 2].astype(F32)
        return w[:, : 3 * D], w[:, 3 * D : 4 * D], w[:, 4 * D : 4 * D + ff], outward, gain[:, 0], gain[:, 1]

    ids = token_ids.reshape(1, tokens)
    ids = jnp.concatenate([ids] + [sw(ids, m) for m in range(1, n)], axis=0)
    ids = jnp.concatenate([ids] + [sw(ids, m * n) for m in range(1, geo.b)], axis=0)
    target = me ^ jnp.array(geo.order, jnp.int32)
    t_seq = (target % n) // r
    t_rank = (target // n) * r + target % r
    halves = jnp.stack([t_rank, 2 * n - 1 - t_rank], axis=1)
    source = (t_seq[:, None] * n + halves // 2) ^ me
    ids = jnp.take(ids.reshape(2 * count, half), (source * 2 + halves % 2).reshape(-1), axis=0).reshape(-1)

    vocab = embedding.shape[0]
    table = jnp.concatenate([embedding, sw(embedding, core)], axis=0)
    line = jnp.arange(vocab, dtype=jnp.int32)
    names = jnp.concatenate([me * vocab + line, (me ^ core) * vocab + line])
    near = ids[: ids.shape[0] // 2]
    picked = mm((near[:, None] == names[None, :]).astype(BF16), table).astype(BF16)
    picked = picked.reshape(len(geo.plane), -1, D)
    row = picked[0]
    for k in range(1, len(geo.plane)):
        row = row + sw(picked[k], geo.plane[k])
    row = row.reshape(len(geo.zs), tokens, D)
    stream = row[0]
    for k in range(1, len(geo.zs)):
        stream = stream + sw(row[k], geo.zs[k])
    stream = stream.astype(F32)

    def half_moves(parity):
        moves = []
        for b in range(geo.b):
            for block in range(n):
                h = 2 * block + parity
                to = geo.device(b, h if h < n else 2 * n - 1 - h)
                moves.append((b * n + block, to))
        return moves

    flat = cotangent.reshape(tokens, D)
    evens = lax.ppermute(flat[:half], AXES, half_moves(0))
    odds = lax.ppermute(flat[half:], AXES, half_moves(1))
    even_rank = rank % 2 == 0
    grad_stream = jnp.where(
        even_rank, jnp.concatenate([evens, odds], axis=0), jnp.concatenate([odds, evens], axis=0)
    ).astype(F32)

    near_masks = list(geo.plane)
    masks = [geo.rank_mask(m) for m in near_masks] + [geo.rank_mask(m ^ core) for m in near_masks]
    spread_pre = [jnp.repeat(mix_pre[l].T, E, axis=1) * E ** (-0.5) for l in range(LAYERS)]
    spread_post = [jnp.repeat(mix_post[l], E, axis=1) for l in range(LAYERS)]

    saved = []
    for l in range(LAYERS):
        qkv, proj, inward, outward, gain_a, gain_f = layer_weights(l)
        n1 = (stream * norm_parts(stream) * gain_a).astype(BF16)
        projected = mm(n1, qkv).astype(BF16)
        queries = projected[:, :D]
        own = projected[:, D:]
        pieces = [own] + [sw(own, m) for m in near_masks[1:]]
        pieces = pieces + [sw(piece, core) for piece in pieces]
        attended, lse, pv = attend(masks, rank_arg, queries, pieces, spread_pre[l], spread_post[l])
        middle = stream + mm(attended, proj)
        n2 = (middle * norm_parts(middle) * gain_f).astype(BF16)
        hidden = mm(n2, inward)
        active = jax.nn.gelu(hidden, approximate=True).astype(BF16)
        saved.append((stream, n1, queries, pieces, attended, lse, pv, middle, n2, hidden, active))
        stream = middle + mm(active, outward)

    final = stream.astype(BF16)
    back_even = [(b, a) for a, b in half_moves(0)]
    back_odd = [(b, a) for a, b in half_moves(1)]
    first = jnp.where(even_rank, final[:half], final[half:])
    second = jnp.where(even_rank, final[half:], final[:half])
    output = jnp.concatenate(
        [lax.ppermute(first, AXES, back_even), lax.ppermute(second, AXES, back_odd)], axis=0
    ).reshape(cotangent.shape)

    shares = [None] * LAYERS
    mixes = [None] * LAYERS
    for l in reversed(range(LAYERS)):
        qkv, proj, inward, outward, gain_a, gain_f = layer_weights(l)
        stream_in, n1, queries, pieces, attended, lse, pv, middle, n2, hidden, active = saved[l]
        gf = grad_stream.astype(BF16)
        back_grad = t_mm(active, gf)
        pull = jax.vjp(lambda z: jax.nn.gelu(z, approximate=True), hidden)[1]
        gz = pull(mm_t(gf, outward))[0].astype(BF16)
        in_grad = t_mm(n2, gz)
        delta, gain_f_grad = norm_back(middle, gain_f, mm_t(gz, inward))
        middle_grad = grad_stream + delta
        gy = middle_grad.astype(BF16)
        proj_grad = t_mm(attended, gy)
        go = mm_t(gy, proj).astype(BF16)
        gq, pre_grad, post_grad, parts = attend_back(
            masks, rank_arg, queries, go, lse, pv, pieces, spread_pre[l], spread_post[l]
        )
        mixes[l] = (pre_grad, post_grad)
        size = len(near_masks)
        sums = [parts[k].astype(F32) + sw(parts[size + k], core).astype(F32) for k in range(size)]
        kv_grad = sums[0]
        for k in range(1, size):
            kv_grad = kv_grad + sw(sums[k].astype(BF16), near_masks[k]).astype(F32)
        joint = jnp.concatenate([gq, kv_grad.astype(BF16)], axis=1)
        qkv_grad = t_mm(n1, joint)
        delta, gain_a_grad = norm_back(stream_in, gain_a, mm_t(joint, qkv))
        grad_stream = middle_grad + delta
        back_cols = back_grad.reshape(folds, D, D)
        gain_cols = jnp.pad(jnp.stack([gain_a_grad, gain_f_grad], axis=1), ((0, 0), (0, 126)))
        packed = jnp.concatenate(
            [qkv_grad.astype(BF16), proj_grad.astype(BF16), in_grad.astype(BF16)]
            + [back_cols[a].astype(BF16) for a in range(folds)]
            + [gain_cols.astype(BF16)],
            axis=1,
        )
        shares[l] = lax.psum_scatter(packed, AXES, scatter_dimension=0, tiled=True).astype(F32)

    g0 = grad_stream.astype(BF16)
    rows = jnp.concatenate([g0] + [sw(g0, m) for m in geo.zs[1:]], axis=0)
    blocks = [rows] + [sw(rows, m) for m in geo.plane[1:]]
    blocks = blocks + [sw(block, core) for block in blocks]
    own_names = me * vocab + line
    embedding_grad = mm(
        (own_names[:, None] == ids[None, :]).astype(BF16), jnp.concatenate(blocks, axis=0)
    )

    pre_sum = jnp.stack([mixes[l][0] for l in range(LAYERS)]).reshape(LAYERS, H, H, E).sum(-1)
    post_sum = jnp.stack([mixes[l][1] for l in range(LAYERS)]).reshape(LAYERS, H, H, E).sum(-1)
    mix = jnp.stack([pre_sum.transpose(0, 2, 1) * E ** (-0.5), post_sum])
    bit = 1
    while bit < count:
        mix = mix + sw(mix, bit)
        bit *= 2

    def in_order(packed):
        part = packed[:, 4 * D : 4 * D + ff]
        return part.reshape(share, folds, count, share).transpose(0, 2, 1, 3).reshape(share, ff)

    def back_order(packed):
        part = packed[:, 4 * D + ff : width]
        return part.reshape(share, folds, D).transpose(1, 0, 2).reshape(back_share, D)

    return (
        output,
        embedding_grad,
        jnp.stack([s[:, width] for s in shares]),
        jnp.stack([s[:, : 3 * D] for s in shares]),
        jnp.stack([s[:, 3 * D : 4 * D] for s in shares]),
        jnp.stack([s[:, width + 1] for s in shares]),
        jnp.stack([in_order(s) for s in shares]),
        jnp.stack([back_order(s) for s in shares]),
        mix[0],
        mix[1],
    )


def solution(mesh):
    everywhere = ("batch", "seq")
    weight = P(None, everywhere, None)
    vector = P(None, everywhere)
    return jax.shard_map(
        functools.partial(shards, Geometry(mesh)),
        mesh=mesh,
        in_specs=(
            P("batch", "seq"),
            P(everywhere, None),
            vector,
            weight,
            weight,
            vector,
            weight,
            weight,
            P(),
            P(),
            P("batch", "seq", None),
        ),
        out_specs=(
            P("batch", "seq", None),
            P(everywhere, None),
            vector,
            weight,
            weight,
            vector,
            weight,
            weight,
            P(),
            P(),
        ),
        check_vma=False,
    )
```

```python
import functools

import jax
import jax.numpy as jnp
from jax import lax
from jax.experimental import pallas as pl
from jax.experimental.pallas import tpu as pltpu
from jax.sharding import PartitionSpec as P

D = 768
H = 12
E = 64
LAYERS = 2
AXES = ("batch", "seq")
NEGATIVE = -1e30
CHUNK = 256
F32 = jnp.float32
BF16 = jnp.bfloat16


class Geometry:
    def __init__(self, mesh):
        self.b = mesh.shape["batch"]
        self.n = mesh.shape["seq"]
        self.r = self.n // self.b
        self.count = self.b * self.n
        self.core = self.n
        low = list(range(self.r))
        self.high = [k * self.n for k in range(0, self.b, 2)]
        self.low = low
        self.plane = [h + l for h in self.high for l in low]
        self.zs = [k * self.r for k in range(self.b)]
        self.order = [c + h + l + z for c in (0, self.core) for h in self.high for l in low for z in self.zs]
        z_bits = bits(self.r, self.n)[::-1]
        x_bits = [bit for bit in bits(self.n, self.count) if bit != self.core]
        y_bits = bits(1, self.r)
        self.x_last = z_bits + y_bits + x_bits + [self.core]
        self.y_last = z_bits + x_bits + y_bits + [self.core]

    def rank_mask(self, mask):
        return (mask // self.n) * self.r + mask % self.n

    def device(self, sequence, rank):
        return (rank // self.r) * self.n + sequence * self.r + rank % self.r


def bits(first, end):
    found = []
    while first < end:
        found.append(first)
        first *= 2
    return found


def reached(masks):
    order = [0]
    for mask in masks:
        order = order + [o ^ mask for o in order]
    return order


def swap(value, mask, count):
    return lax.ppermute(value, AXES, [(p, p ^ mask) for p in range(count)])


def dot(a, b, contract):
    return lax.dot_general(a, b, (contract, ((), ())), preferred_element_type=F32)


def load_keys(sources, n, half, rank, pieces, kv, sems):
    copies = []
    for k, (index, row, mask, part) in enumerate(sources):
        owner = rank ^ mask
        place = owner if part == 0 else 2 * n - 1 - owner
        copies.append(
            pltpu.make_async_copy(
                pieces[index].at[pl.ds(row, half)],
                kv.at[pl.ds(pl.multiple_of(place * half, half), half)],
                sems.at[k],
            )
        )
    for copy in copies:
        copy.start()
    return copies


def mixed_rows(rows, weights):
    return jnp.concatenate([rows * weights[g : g + 1, :] for g in range(H)], axis=0)


def forward_kernel(n, sources, count, half, rank_ref, q_ref, pre_ref, post_ref, *rest):
    pieces = rest[:count]
    o_ref, lse_ref, pv_ref = rest[count : count + 3]
    kv, qg, logits, top, total, acc, sems = rest[count + 3 :]
    rank = rank_ref[0]
    rows = H * half
    copies = load_keys(sources, n, half, rank, pieces, kv, sems)
    for copy in copies:
        copy.wait()
    for part in range(2):
        place = rank if part == 0 else 2 * n - 1 - rank
        live = (place * half + half + CHUNK - 1) // CHUNK
        q_part = q_ref[part * half : (part + 1) * half, :].astype(F32)
        qg[...] = mixed_rows(q_part, pre_ref[...]).astype(BF16)
        top[...] = jnp.full((rows, 128), NEGATIVE, F32)
        total[...] = jnp.zeros((rows, 128), F32)
        acc[...] = jnp.zeros((rows, D), F32)
        spot = place * half + lax.broadcasted_iota(jnp.int32, (rows, CHUNK), 0) % half
        lane = lax.broadcasted_iota(jnp.int32, (rows, CHUNK), 1)

        def score(c, carry):
            start = pl.multiple_of(c * CHUNK, CHUNK)
            found = dot(qg[...], kv[pl.ds(start, CHUNK), :D], ((1,), (1,)))
            found = jnp.where(start + lane <= spot, found, NEGATIVE)
            logits[c] = found
            best = found[:, :128]
            for k in range(1, CHUNK // 128):
                best = jnp.maximum(best, found[:, k * 128 : (k + 1) * 128])
            top[...] = jnp.maximum(top[...], best)
            return carry

        lax.fori_loop(0, live, score, 0)
        row_max = jnp.max(top[...], axis=1, keepdims=True)

        def weigh(c, carry):
            start = pl.multiple_of(c * CHUNK, CHUNK)
            prob = jnp.exp(logits[c] - row_max)
            part_sum = prob[:, :128]
            for k in range(1, CHUNK // 128):
                part_sum = part_sum + prob[:, k * 128 : (k + 1) * 128]
            total[...] += part_sum
            acc[...] += dot(prob.astype(BF16), kv[pl.ds(start, CHUNK), D:], ((1,), (0,)))
            return carry

        lax.fori_loop(0, live, weigh, 0)
        row_sum = jnp.sum(total[...], axis=1, keepdims=True)
        scale = 1.0 / row_sum
        lse = jnp.broadcast_to(row_max + jnp.log(row_sum), (rows, 128))
        lse_ref[part] = jnp.transpose(lse)[:8, :]
        out = jnp.zeros((half, D), F32)
        for g in range(H):
            normal = acc[g * half : (g + 1) * half, :] * scale[g * half : (g + 1) * half, :]
            pv_ref[part, g * half : (g + 1) * half, :] = normal.astype(BF16)
            out = out + normal * post_ref[g : g + 1, :]
        o_ref[part * half : (part + 1) * half, :] = out.astype(BF16)


def backward_kernel(n, sources, count, masks, half, rank_ref, q_ref, go_ref, lse_ref, pv_ref, pre_ref, post_ref, *rest):
    pieces = rest[:count]
    gq_ref, pre_grad_ref, post_grad_ref = rest[count : count + 3]
    grads = rest[count + 3 : count + 3 + n]
    kv, qg, gg, gk, gv, acc, sems, out_sems = rest[count + 3 + n :]
    rank = rank_ref[0]
    rows = H * half
    copies = load_keys(sources, n, half, rank, pieces, kv, sems)
    gk[...] = jnp.zeros(gk.shape, F32)
    gv[...] = jnp.zeros(gv.shape, F32)
    pre_grad_ref[...] = jnp.zeros(pre_grad_ref.shape, F32)
    post_grad_ref[...] = jnp.zeros(post_grad_ref.shape, F32)
    for copy in copies:
        copy.wait()
    for part in range(2):
        place = rank if part == 0 else 2 * n - 1 - rank
        live = (place * half + half + CHUNK - 1) // CHUNK
        q_part = q_ref[part * half : (part + 1) * half, :].astype(F32)
        go_part = go_ref[part * half : (part + 1) * half, :].astype(F32)
        row_dots = []
        for g in range(H):
            qg[g * half : (g + 1) * half, :] = (q_part * pre_ref[g : g + 1, :]).astype(BF16)
            mixed = go_part * post_ref[g : g + 1, :]
            gg[g * half : (g + 1) * half, :] = mixed.astype(BF16)
            normal = pv_ref[part, g * half : (g + 1) * half, :].astype(F32)
            row_dots.append(jnp.sum(mixed * normal, axis=1, keepdims=True))
            post_grad_ref[g : g + 1, :] += jnp.sum(go_part * normal, axis=0, keepdims=True)
        row_dot = jnp.broadcast_to(jnp.concatenate(row_dots, axis=0), (rows, 128))
        row_dot = jnp.transpose(row_dot)[:1, :]
        lse = lse_ref[part][:1, :]
        acc[...] = jnp.zeros((rows, D), F32)
        spot = place * half + lax.broadcasted_iota(jnp.int32, (CHUNK, rows), 1) % half
        line = lax.broadcasted_iota(jnp.int32, (CHUNK, rows), 0)

        def block(c, carry):
            start = pl.multiple_of(c * CHUNK, CHUNK)
            keys = kv[pl.ds(start, CHUNK), :D]
            values = kv[pl.ds(start, CHUNK), D:]
            found = dot(keys, qg[...], ((1,), (1,)))
            found = jnp.where(start + line <= spot, found, NEGATIVE)
            prob = jnp.exp(found - lse)
            grad_prob = dot(values, gg[...], ((1,), (1,)))
            grad_logit = (prob * (grad_prob - row_dot)).astype(BF16)
            gv[pl.ds(start, CHUNK), :] += dot(prob.astype(BF16), gg[...], ((1,), (0,)))
            gk[pl.ds(start, CHUNK), :] += dot(grad_logit, qg[...], ((1,), (0,)))
            acc[...] += dot(grad_logit, keys, ((0,), (0,)))
            return carry

        lax.fori_loop(0, live, block, 0)
        gq = jnp.zeros((half, D), F32)
        for g in range(H):
            found = acc[g * half : (g + 1) * half, :]
            gq = gq + found * pre_ref[g : g + 1, :]
            pre_grad_ref[g : g + 1, :] += jnp.sum(found * q_part, axis=0, keepdims=True)
        gq_ref[part * half : (part + 1) * half, :] = gq.astype(BF16)
    kv[:, :D] = gk[...].astype(BF16)
    kv[:, D:] = gv[...].astype(BF16)
    copies = []
    for index, mask in enumerate(masks):
        owner = rank ^ mask
        for part, place in ((0, owner), (1, 2 * n - 1 - owner)):
            start = pl.multiple_of(place * half, half)
            copies.append(
                pltpu.make_async_copy(
                    kv.at[pl.ds(start, half)],
                    grads[index].at[pl.ds(part * half, half)],
                    out_sems.at[2 * index + part],
                )
            )
    for copy in copies:
        copy.start()
    for copy in copies:
        copy.wait()


VMEM = pl.BlockSpec(memory_space=pltpu.VMEM)
SMEM = pl.BlockSpec(memory_space=pltpu.SMEM)
ANY = pl.BlockSpec(memory_space=pl.ANY)
LIMIT = pltpu.CompilerParams(vmem_limit_bytes=58 * 2**20)


def attend(n, sources, rank, queries, pieces, pre, post):
    count = len(pieces)
    tokens = queries.shape[0]
    half = tokens // 2
    rows = H * half
    length = n * tokens
    return pl.pallas_call(
        functools.partial(forward_kernel, n, sources, count, half),
        out_shape=(
            jax.ShapeDtypeStruct((tokens, D), BF16),
            jax.ShapeDtypeStruct((2, 8, rows), F32),
            jax.ShapeDtypeStruct((2, rows, D), BF16),
        ),
        in_specs=[SMEM, VMEM, VMEM, VMEM] + [ANY] * count,
        out_specs=(VMEM, VMEM, VMEM),
        scratch_shapes=[
            pltpu.VMEM((length, 2 * D), BF16),
            pltpu.VMEM((rows, D), BF16),
            pltpu.VMEM((length // CHUNK, rows, CHUNK), F32),
            pltpu.VMEM((rows, 128), F32),
            pltpu.VMEM((rows, 128), F32),
            pltpu.VMEM((rows, D), F32),
            pltpu.SemaphoreType.DMA((2 * n,)),
        ],
        compiler_params=LIMIT,
        cost_estimate=pl.CostEstimate(flops=10**10, bytes_accessed=8 * 2**20, transcendentals=2**20),
        name="attend",
    )(rank, queries, pre, post, *pieces)


def attend_back(sources, masks, rank, queries, grad_out, lse, pv, pieces, pre, post):
    n = len(masks)
    count = len(pieces)
    tokens = queries.shape[0]
    half = tokens // 2
    rows = H * half
    length = n * tokens
    outs = pl.pallas_call(
        functools.partial(backward_kernel, n, sources, count, masks, half),
        out_shape=(
            jax.ShapeDtypeStruct((tokens, D), BF16),
            jax.ShapeDtypeStruct((H, D), F32),
            jax.ShapeDtypeStruct((H, D), F32),
        )
        + tuple(jax.ShapeDtypeStruct((tokens, 2 * D), BF16) for _ in masks),
        in_specs=[SMEM] + [VMEM] * 6 + [ANY] * count,
        out_specs=(VMEM, VMEM, VMEM) + (ANY,) * n,
        scratch_shapes=[
            pltpu.VMEM((length, 2 * D), BF16),
            pltpu.VMEM((rows, D), BF16),
            pltpu.VMEM((rows, D), BF16),
            pltpu.VMEM((length, D), F32),
            pltpu.VMEM((length, D), F32),
            pltpu.VMEM((rows, D), F32),
            pltpu.SemaphoreType.DMA((2 * n,)),
            pltpu.SemaphoreType.DMA((2 * n,)),
        ],
        compiler_params=LIMIT,
        cost_estimate=pl.CostEstimate(flops=16 * 10**9, bytes_accessed=12 * 2**20, transcendentals=2**20),
        name="attend_back",
    )(rank, queries, grad_out, lse, pv, pre, post, *pieces)
    return outs[0], outs[1], outs[2], outs[3:]


def mm(a, b):
    return jnp.dot(a, b, preferred_element_type=F32)


def mm_t(a, b):
    return lax.dot_general(a, b, (((1,), (1,)), ((), ())), preferred_element_type=F32)


def t_mm(a, b):
    return lax.dot_general(a, b, (((0,), (0,)), ((), ())), preferred_element_type=F32)


def norm_parts(x):
    return lax.rsqrt(jnp.mean(x * x, axis=-1, keepdims=True) + 1e-06)


def norm_back(x, gain, grad):
    r = norm_parts(x)
    gain_grad = jnp.sum(grad * x * r, axis=0)
    scaled = grad * gain
    x_grad = r * scaled - x * (r * r * r) * jnp.mean(scaled * x, axis=-1, keepdims=True)
    return x_grad, gain_grad


def shards(
    geo,
    token_ids,
    embedding,
    gain_attn,
    w_qkv,
    w_proj,
    gain_ffn,
    w_in,
    w_back,
    mix_pre,
    mix_post,
    cotangent,
):
    n, r, count, core = geo.n, geo.r, geo.count, geo.core
    tokens = token_ids.size
    half = tokens // 2
    i = lax.axis_index("batch")
    j = lax.axis_index("seq")
    me = i * n + j
    rank = i * r + j % r
    rank_arg = rank.reshape(1).astype(jnp.int32)
    share = w_qkv.shape[1]
    back_share = w_back.shape[1]
    folds = back_share // share
    ff = w_in.shape[2]
    sw = functools.partial(swap, count=count)

    def packed_in(l):
        return w_in[l].reshape(share, count, folds, share).transpose(0, 2, 1, 3).reshape(share, ff)

    def packed_back(l):
        return jnp.concatenate([w_back[l, a * share : (a + 1) * share] for a in range(folds)], axis=1)

    gains = jnp.stack([gain_attn[0], gain_ffn[0], gain_attn[1], gain_ffn[1]], axis=1)
    gains = jnp.pad(gains, ((0, 0), (0, 124)))
    wide = [w_qkv[0], w_proj[0], gains]
    pairs = [
        jnp.concatenate(wide + [packed_in(0), packed_back(0)][:1], axis=1),
        jnp.concatenate([packed_back(0), w_qkv[1], w_proj[1]], axis=1),
        jnp.concatenate([packed_in(1), packed_back(1)], axis=1),
    ]
    borders = [4 * D + gains.shape[1], folds * D, ff]
    routes = [geo.x_last, geo.y_last]
    shared = len(geo.zs).bit_length() - 1
    stages = len(geo.x_last) - 1
    timed = stages == 4
    split = [None] * len(pairs)
    last_round = [None]

    def begin_round(number, after, late=None):
        pending = []
        for p in range(len(pairs)):
            k = number - 2 * p
            if 0 <= k < shared:
                pending.append((p, None, geo.x_last[k], pairs[p]))
            elif shared <= k < stages:
                if k == shared:
                    split[p] = [pairs[p][:, : borders[p]], pairs[p][:, borders[p] :]]
                pending += [(p, side, routes[side][k], split[p][side]) for side in range(2)]
        values = [entry[3] for entry in pending]
        if timed:
            values = list(lax.optimization_barrier((values, after, last_round[0]))[0])
            if late is not None:
                values[late[0]], _ = lax.optimization_barrier((values[late[0]], late[1]))
        arrived = [sw(value, entry[2]) for value, entry in zip(values, pending)]
        last_round[0] = arrived
        return pending, values, arrived

    def end_round(state, hold):
        pending, values, arrived = state
        if timed and hold is not None:
            arrived = lax.optimization_barrier((arrived, hold))[0]
            last_round[0] = arrived
        for value, there, (p, side, _, _) in zip(values, arrived, pending):
            joined = jnp.concatenate([value, there], axis=0)
            if side is None:
                pairs[p] = joined
            else:
                split[p][side] = joined

    ids = token_ids.reshape(1, tokens)
    ids = jnp.concatenate([ids] + [sw(ids, m * n) for m in range(1, geo.b)], axis=0)
    first_ids = ids
    ids = jnp.stack([ids] + [sw(ids, m) for m in range(1, n)], axis=1)
    target = me ^ jnp.array(geo.order, jnp.int32)
    t_seq = (target % n) // r
    t_rank = (target // n) * r + target % r
    halves = jnp.stack([t_rank, 2 * n - 1 - t_rank], axis=1)
    source = (t_seq[:, None] * n + halves // 2) ^ me
    ids = jnp.take(ids.reshape(2 * count, half), (source * 2 + halves % 2).reshape(-1), axis=0).reshape(-1)

    vocab = embedding.shape[0]
    line = jnp.arange(vocab, dtype=jnp.int32)
    table, first_ids = lax.optimization_barrier((embedding, first_ids))
    tables = [table] + [sw(table, m) for m in geo.high[1:]]
    tables = tables + [sw(part, core) for part in tables]
    owners = geo.high + [m ^ core for m in geo.high]
    end_round(begin_round(0, first_ids), None)
    end_round(begin_round(1, first_ids), None)
    third = begin_round(2, first_ids)
    near = ids[: len(geo.low) * len(geo.zs) * tokens]
    picked = jnp.zeros((near.shape[0], D), F32)
    for m, part in zip(owners, tables):
        picked = picked + mm((near[:, None] == ((me ^ m) * vocab + line)[None, :]).astype(BF16), part)
    picked = picked.astype(BF16)
    end_round(third, picked)
    flat = picked.reshape(len(geo.low), -1, D)
    row = flat[0]
    for k in range(1, len(geo.low)):
        row = row + sw(flat[k], geo.low[k])
    fourth = begin_round(3, picked, (1, row))
    row = row.reshape(len(geo.zs), tokens, D)
    stream = row[0]
    for k in range(1, len(geo.zs)):
        stream = stream + sw(row[k], geo.zs[k])
    stream = stream.astype(F32)
    end_round(fourth, stream)
    fifth = begin_round(4, stream)
    if not timed:
        end_round(fifth, None)
        for number in range(5, stages + 2 * len(pairs) - 2):
            end_round(begin_round(number, None), None)

    side = D // 2
    feature = jnp.arange(D, dtype=jnp.int32)

    def turner(route):
        order = jnp.repeat(jnp.array(reached(route), jnp.int32), share)
        origin = (me ^ order) * share + feature % share
        return (feature[:, None] == origin[None, :]).astype(BF16)

    turn_x, turn_y = turner(geo.x_last), turner(geo.y_last)

    def relative(value, turn):
        turned = mm(value, turn).astype(BF16)
        return turned[:, :side], turned[:, side:]

    def times(value, pair, start, width):
        near, far = pair
        return mm(value[0], near[:, start : start + width]) + mm(value[1], far[:, start : start + width])

    def back_times(value, pair, start, width, turn):
        near, far = pair
        near, far = (mm_t(value, side[:, start : start + width]).astype(BF16) for side in (near, far))
        return mm_t(jnp.concatenate([near, far], axis=1), turn)

    def finish(p):
        return [(value, sw(value, core)) for value in split[p]]

    turns = [turn_x, turn_y]
    attns, inwards, outwards = [None] * LAYERS, [None] * LAYERS, [None] * LAYERS
    attns[0], inwards[0] = finish(0)
    gain_all = jnp.concatenate([side[:, 4 * D : 4 * D + 8] for side in attns[0]], axis=0)
    gain_all = mm(turn_x, gain_all).T

    class Sum:
        def __init__(self, value, route):
            self.value = value
            self.masks = list(route[:-2])

        def outgoing(self):
            if not self.masks:
                return []
            return [(self.value[self.value.shape[0] // 2 :], self.masks.pop())]

        def incoming(self, arrived):
            for there in arrived:
                rows = self.value.shape[0] // 2
                self.value = self.value[:rows].astype(F32) + there.astype(F32)
                if self.masks:
                    self.value = self.value.astype(BF16)

        def step(self):
            self.incoming([sw(value, mask) for value, mask in self.outgoing()])

        def result(self):
            while self.masks:
                self.step()
            return self.value

    def exchange(after, sums, others=()):
        entries = list(others)
        spans = []
        for one in sums:
            out = one.outgoing()
            spans.append(len(out))
            entries += out
        values = lax.optimization_barrier(([value for value, _ in entries], after))[0]
        arrived = [sw(value, mask) for value, (_, mask) in zip(values, entries)]
        arrived = list(lax.optimization_barrier(arrived))
        place = len(others)
        for one, span in zip(sums, spans):
            one.incoming(arrived[place : place + span])
            place += span
        return arrived[: len(others)]

    def tie(value, sums):
        value, held_sums = lax.optimization_barrier((value, [one.value for one in sums]))
        for one, held_sum in zip(sums, held_sums):
            one.value = held_sum
        return value

    x_mask = geo.x_last[-2]
    quarter = D // 4
    quarters = [turn_x[:, k * quarter : (k + 1) * quarter] for k in range(4)]

    rows_of = [
        (i ^ (m // n)) * quarter + jnp.arange(quarter, dtype=jnp.int32) for m in (0, x_mask, core, x_mask ^ core)
    ]
    straight = [(feature[:, None] == rows[None, :]).astype(BF16) for rows in rows_of]

    def four_rows(values, quarters):
        tall = jnp.concatenate(values, axis=0)
        stay, to_x, to_core, to_both = (mm(tall, q).astype(BF16) for q in quarters)
        size = tall.shape[0]
        from_x = sw(jnp.concatenate([to_x, to_both], axis=0), x_mask)
        rest = sw(jnp.concatenate([to_core, from_x[size:]], axis=0), core)
        spots = [slice(k * tokens, (k + 1) * tokens) for k in range(len(values))]
        return [
            jnp.concatenate([stay[s], from_x[:size][s], rest[:size][s], rest[size:][s]], axis=0) for s in spots
        ]

    def two_tokens(value):
        return jnp.concatenate([value, sw(value, x_mask)], axis=0)

    def four_tokens(value):
        return jnp.concatenate([value, sw(value, core)], axis=0)

    def side_by_side(parts):
        return jnp.concatenate([part.astype(BF16) for part in parts], axis=1)

    def fold(value, a):
        return tuple(side[a * tokens : (a + 1) * tokens] for side in value)

    def half_moves(parity):
        moves = []
        for b in range(geo.b):
            for block in range(n):
                h = 2 * block + parity
                to = geo.device(b, h if h < n else 2 * n - 1 - h)
                moves.append((b * n + block, to))
        return moves

    flat = cotangent.reshape(tokens, D)
    evens = lax.ppermute(flat[:half], AXES, half_moves(0))
    odds = lax.ppermute(flat[half:], AXES, half_moves(1))
    even_rank = rank % 2 == 0
    grad_stream = jnp.where(
        even_rank, jnp.concatenate([evens, odds], axis=0), jnp.concatenate([odds, evens], axis=0)
    ).astype(F32)

    near_masks = list(geo.plane)
    masks = [geo.rank_mask(m) for m in near_masks] + [geo.rank_mask(m ^ core) for m in near_masks]
    if len(near_masks) == 4:
        near_sources = [(k, part * half, m, part) for k, m in enumerate(masks[:3]) for part in range(2)]
        near_sources += [(3, 0, masks[3], 0), (4, 0, masks[3], 1)]
    else:
        near_sources = [(k, part * half, m, part) for k, m in enumerate(masks[:n // 2]) for part in range(2)]
    piece_count = near_sources[-1][0] + 1
    sources = near_sources + [
        (k + piece_count, row, m ^ geo.rank_mask(core), part) for k, row, m, part in near_sources
    ]

    spread_pre = [jnp.repeat(mix_pre[l].T, E, axis=1) * E ** (-0.5) for l in range(LAYERS)]
    spread_post = [jnp.repeat(mix_post[l], E, axis=1) for l in range(LAYERS)]

    def spread_keys(own):
        if len(near_masks) == 4:
            y, x = near_masks[1], near_masks[2]
            by_y, by_x = sw(own, y), sw(own, x)
            return [own, by_y, by_x, sw(by_x[:half], y), sw(by_y[half:], x)]
        return [own] + [sw(own, m) for m in near_masks[1:]]

    saved = []
    for l in range(LAYERS):
        gain_a, gain_f = gain_all[2 * l], gain_all[2 * l + 1]
        turn = turns[l]
        n1 = (stream * norm_parts(stream) * gain_a).astype(BF16)
        projected = times(relative(n1, turn), attns[l], 0, 3 * D).astype(BF16)
        queries = projected[:, :D]
        if timed and l == 0:
            end_round(fifth, projected)
            sixth = begin_round(5, projected)
        pieces = spread_keys(projected[:, D:])
        pieces = pieces + [sw(piece, core) for piece in pieces]
        attended, lse, pv = attend(n, sources, rank_arg, queries, pieces, spread_pre[l], spread_post[l])
        if timed:
            end_round(sixth if l == 0 else eighth, attended)
        if l == 0:
            if timed:
                seventh = begin_round(6, attended)
            outwards[0], attns[1] = finish(1)
        else:
            inwards[1], outwards[1] = finish(2)
        middle = stream + times(relative(attended, turn), attns[l], 3 * D, D)
        n2 = (middle * norm_parts(middle) * gain_f).astype(BF16)
        hidden = times(relative(n2, turns[1 - l]), inwards[l], 0, ff)
        active = jax.nn.gelu(hidden, approximate=True).astype(BF16)
        wide = relative(jnp.concatenate([active[:, a * D : (a + 1) * D] for a in range(folds)], axis=0), turns[l])
        stream_in, stream = stream, middle
        for a in range(folds):
            stream = stream + times(fold(wide, a), outwards[l], a * D, D)
        if timed and l == 0:
            end_round(seventh, stream)
            eighth = begin_round(7, stream)
        saved.append((stream_in, n1, queries, pieces, attended, lse, pv, middle, n2, hidden, active, wide))

    final = stream.astype(BF16)
    back_even = [(b, a) for a, b in half_moves(0)]
    back_odd = [(b, a) for a, b in half_moves(1)]
    first = jnp.where(even_rank, final[:half], final[half:])
    second = jnp.where(even_rank, final[half:], final[:half])
    output = jnp.concatenate(
        [lax.ppermute(first, AXES, back_even), lax.ppermute(second, AXES, back_odd)], axis=0
    ).reshape(cotangent.shape)

    shares = [None] * LAYERS
    mixes = [None] * LAYERS
    gain_grads = [None] * LAYERS
    for l in reversed(range(LAYERS)):
        gain_a, gain_f = gain_all[2 * l], gain_all[2 * l + 1]
        stream_in, n1, queries, pieces, attended, lse, pv, middle, n2, hidden, active, wide = saved[l]
        gf = grad_stream.astype(BF16)
        pull = jax.vjp(lambda z: jax.nn.gelu(z, approximate=True), hidden)[1]
        active_grad = [back_times(gf, outwards[l], a * D, D, turns[l]) for a in range(folds)]
        gz = pull(jnp.concatenate(active_grad, axis=1))[0].astype(BF16)
        normed_grad = back_times(gz, inwards[l], 0, ff, turns[1 - l])
        gf_four = four_tokens(two_tokens(gf))
        tall = four_rows([active[:, a * D : (a + 1) * D] for a in range(folds)] + [n2, attended], straight)
        back_grad = [t_mm(part, gf_four) for part in tall[:folds]]
        if l == 0:
            (tall_n1,) = four_rows([n1], quarters)
        else:
            gz_two = two_tokens(gz)
        delta, gain_f_grad = norm_back(middle, gain_f, normed_grad)
        middle_grad = grad_stream + delta
        gy = middle_grad.astype(BF16)
        go = back_times(gy, attns[l], 3 * D, D, turns[l]).astype(BF16)
        if l == 0:
            gz_two = two_tokens(jnp.concatenate([gz, gy], axis=1))
            go, attn_grad, back_grad = lax.optimization_barrier((go, attn_grad, back_grad))
        gq, pre_grad, post_grad, parts = attend_back(
            sources, masks, rank_arg, queries, go, lse, pv, pieces, spread_pre[l], spread_post[l]
        )
        mixes[l] = (pre_grad, post_grad)
        size = len(near_masks)
        sums = [parts[k].astype(F32) + sw(parts[size + k], core).astype(F32) for k in range(size)]
        others = [(sums[k].astype(BF16), near_masks[k]) for k in range(1, size)]
        arrived = [sw(value, mask) for value, mask in others]
        gz_two, _ = lax.optimization_barrier((gz_two, sums))
        gz_four = four_tokens(gz_two)
        if l == 0:
            pack = attn_grad + back_grad + [t_mm(tall[folds], gz_four[:, :ff]), t_mm(tall[folds + 1], gz_four[:, ff:])]
        else:
            pack = back_grad + [t_mm(tall[folds], gz_four)]
        pack = side_by_side(pack)
        pack, arrived = lax.optimization_barrier((pack, arrived))
        shares[l] = lax.psum_scatter(pack, "seq", scatter_dimension=0, tiled=True)
        if l == 0:
            shares[1], arrived = lax.optimization_barrier((shares[1], arrived))
        kv_grad = sums[0]
        for there in arrived:
            kv_grad = kv_grad + there.astype(F32)
        joint = jnp.concatenate([gq, kv_grad.astype(BF16)], axis=1)
        normed_grad = back_times(joint, attns[l], 0, 3 * D, turns[l])
        if l == 0:
            joint_zero = joint
        else:
            both = four_tokens(two_tokens(jnp.concatenate([joint, gy], axis=1)))
            (tall_n1,) = four_rows([n1], straight)
            attn_grad = [t_mm(tall_n1, both[:, : 3 * D]), t_mm(tall[folds + 1], both[:, 3 * D :])]
        delta, gain_a_grad = norm_back(stream_in, gain_a, normed_grad)
        grad_stream = middle_grad + delta
        gain_grads[l] = (gain_a_grad, gain_f_grad)

    pre_sum = jnp.stack([mixes[l][0] for l in range(LAYERS)]).reshape(LAYERS, H, H, E).sum(-1)
    post_sum = jnp.stack([mixes[l][1] for l in range(LAYERS)]).reshape(LAYERS, H, H, E).sum(-1)
    small = jnp.concatenate(
        [(pre_sum.transpose(0, 2, 1) * E ** (-0.5)).reshape(-1), post_sum.reshape(-1)]
        + [gain_grads[l][k] for k in range(2) for l in range(LAYERS)]
    )
    size = small.shape[0]
    small = jnp.pad(small, (0, -size % 1024)).reshape(-1, 128)
    small_masks = bits(1, count)

    g0 = grad_stream.astype(BF16)
    arrived = exchange(g0, [], [(joint_zero, x_mask)] + [(g0, m) for m in geo.zs[1:]])
    joint_four = four_tokens(jnp.concatenate([joint_zero, arrived[0]], axis=0))
    qkv_sum = Sum(t_mm(tall_n1, joint_four).astype(BF16), geo.x_last)
    rows = jnp.concatenate([g0] + arrived[1:], axis=0)
    if len(geo.plane) == 4:
        cut = rows.shape[0] // 2
        y, x = geo.plane[1], geo.plane[2]
        by_y, by_x = exchange(rows, [], [(rows, y), (rows, x)])
        both = exchange(by_x, [qkv_sum], [(by_x[:cut], y), (by_y[cut:], x)])
        blocks = [rows, by_y, by_x] + both
    else:
        blocks = [rows] + exchange(rows, [], [(rows, m) for m in geo.plane[1:]])
        exchange(blocks[-1], [qkv_sum])
    blocks = blocks + [sw(block, core) for block in blocks]

    def share_small(after, sums):
        nonlocal small
        (there,) = exchange(after, sums, [(small, small_masks.pop())])
        small = small + there

    share_small(blocks, [qkv_sum])
    own_names = me * vocab + line
    embedding_grad = mm(
        (own_names[:, None] == ids[None, :]).astype(BF16), jnp.concatenate(blocks, axis=0)
    )
    share_small(qkv_sum.value, [qkv_sum])
    while small_masks:
        share_small(qkv_sum.value, [])
    small = small.reshape(-1)[:size]
    mix = small[: 2 * LAYERS * H * H].reshape(2, LAYERS, H, H)
    gain_sum = small[2 * LAYERS * H * H :].reshape(2, LAYERS, D)
    gain_sum = lax.dynamic_slice(gain_sum, (0, 0, me * share), (2, LAYERS, share))

    def in_order(part):
        return part.reshape(share, folds, count, share).transpose(0, 2, 1, 3).reshape(share, ff)

    def back_order(part):
        return jnp.concatenate([part[:, a * D : (a + 1) * D] for a in range(folds)], axis=0)

    qkv_share = qkv_sum.result()
    one, zero = shares[1].astype(F32), shares[0].astype(F32)
    attn_share, zero = zero[:, : 4 * D], zero[:, 4 * D :]
    width = folds * D
    return (
        output,
        embedding_grad,
        gain_sum[0],
        jnp.stack([qkv_share, attn_share[:, : 3 * D]]),
        jnp.stack([zero[:, width + ff :], attn_share[:, 3 * D :]]),
        gain_sum[1],
        jnp.stack([in_order(zero[:, width : width + ff]), in_order(one[:, width:])]),
        jnp.stack([back_order(zero[:, :width]), back_order(one[:, :width])]),
        mix[0],
        mix[1],
    )


def solution(mesh):
    everywhere = ("batch", "seq")
    weight = P(None, everywhere, None)
    vector = P(None, everywhere)
    return jax.shard_map(
        functools.partial(shards, Geometry(mesh)),
        mesh=mesh,
        in_specs=(
            P("batch", "seq"),
            P(everywhere, None),
            vector,
            weight,
            weight,
            vector,
            weight,
            weight,
            P(),
            P(),
            P("batch", "seq", None),
        ),
        out_specs=(
            P("batch", "seq", None),
            P(everywhere, None),
            vector,
            weight,
            weight,
            vector,
            weight,
            weight,
            P(),
            P(),
        ),
        check_vma=False,
    )
```

```python
import functools

import jax
import jax.numpy as jnp
from jax import lax
from jax.experimental import pallas as pl
from jax.experimental.pallas import tpu as pltpu
from jax.sharding import PartitionSpec as P

D = 768
H = 12
E = 64
LAYERS = 2
AXES = ("batch", "seq")
NEGATIVE = -1e30
CHUNK = 256
F32 = jnp.float32
BF16 = jnp.bfloat16


class Geometry:
    def __init__(self, mesh):
        self.b = mesh.shape["batch"]
        self.n = mesh.shape["seq"]
        self.r = self.n // self.b
        self.count = self.b * self.n
        self.core = self.n
        low = list(range(self.r))
        self.high = [k * self.n for k in range(0, self.b, 2)]
        self.low = low
        self.plane = [h + l for h in self.high for l in low]
        self.zs = [k * self.r for k in range(self.b)]
        self.order = [c + h + l + z for c in (0, self.core) for h in self.high for l in low for z in self.zs]
        z_bits = bits(self.r, self.n)[::-1]
        x_bits = [bit for bit in bits(self.n, self.count) if bit != self.core]
        y_bits = bits(1, self.r)
        self.x_last = z_bits + y_bits + x_bits + [self.core]
        self.y_last = z_bits + x_bits + y_bits + [self.core]

    def rank_mask(self, mask):
        return (mask // self.n) * self.r + mask % self.n

    def device(self, sequence, rank):
        return (rank // self.r) * self.n + sequence * self.r + rank % self.r


def bits(first, end):
    found = []
    while first < end:
        found.append(first)
        first *= 2
    return found


def reached(masks):
    order = [0]
    for mask in masks:
        order = order + [o ^ mask for o in order]
    return order


def swap(value, mask, count):
    return lax.ppermute(value, AXES, [(p, p ^ mask) for p in range(count)])


def dot(a, b, contract):
    return lax.dot_general(a, b, (contract, ((), ())), preferred_element_type=F32)


def load_keys(sources, n, half, rank, pieces, kv, sems):
    copies = []
    for k, (index, row, mask, part) in enumerate(sources):
        owner = rank ^ mask
        place = owner if part == 0 else 2 * n - 1 - owner
        copies.append(
            pltpu.make_async_copy(
                pieces[index].at[pl.ds(row, half)],
                kv.at[pl.ds(pl.multiple_of(place * half, half), half)],
                sems.at[k],
            )
        )
    for copy in copies:
        copy.start()
    return copies


def mixed_rows(rows, weights):
    return jnp.concatenate([rows * weights[g : g + 1, :] for g in range(H)], axis=0)


def forward_kernel(n, sources, count, half, rank_ref, q_ref, pre_ref, post_ref, *rest):
    pieces = rest[:count]
    o_ref, lse_ref, pv_ref = rest[count : count + 3]
    kv, qg, logits, top, total, acc, sems = rest[count + 3 :]
    rank = rank_ref[0]
    rows = H * half
    copies = load_keys(sources, n, half, rank, pieces, kv, sems)
    for copy in copies:
        copy.wait()
    for part in range(2):
        place = rank if part == 0 else 2 * n - 1 - rank
        live = (place * half + half + CHUNK - 1) // CHUNK
        q_part = q_ref[part * half : (part + 1) * half, :].astype(F32)
        qg[...] = mixed_rows(q_part, pre_ref[...]).astype(BF16)
        top[...] = jnp.full((rows, 128), NEGATIVE, F32)
        total[...] = jnp.zeros((rows, 128), F32)
        acc[...] = jnp.zeros((rows, D), F32)
        spot = place * half + lax.broadcasted_iota(jnp.int32, (rows, CHUNK), 0) % half
        lane = lax.broadcasted_iota(jnp.int32, (rows, CHUNK), 1)

        def score(c, carry):
            start = pl.multiple_of(c * CHUNK, CHUNK)
            found = dot(qg[...], kv[pl.ds(start, CHUNK), :D], ((1,), (1,)))
            found = jnp.where(start + lane <= spot, found, NEGATIVE)
            logits[c] = found
            best = found[:, :128]
            for k in range(1, CHUNK // 128):
                best = jnp.maximum(best, found[:, k * 128 : (k + 1) * 128])
            top[...] = jnp.maximum(top[...], best)
            return carry

        lax.fori_loop(0, live, score, 0)
        row_max = jnp.max(top[...], axis=1, keepdims=True)

        def weigh(c, carry):
            start = pl.multiple_of(c * CHUNK, CHUNK)
            prob = jnp.exp(logits[c] - row_max)
            part_sum = prob[:, :128]
            for k in range(1, CHUNK // 128):
                part_sum = part_sum + prob[:, k * 128 : (k + 1) * 128]
            total[...] += part_sum
            acc[...] += dot(prob.astype(BF16), kv[pl.ds(start, CHUNK), D:], ((1,), (0,)))
            return carry

        lax.fori_loop(0, live, weigh, 0)
        row_sum = jnp.sum(total[...], axis=1, keepdims=True)
        scale = 1.0 / row_sum
        lse = jnp.broadcast_to(row_max + jnp.log(row_sum), (rows, 128))
        lse_ref[part] = jnp.transpose(lse)[:8, :]
        out = jnp.zeros((half, D), F32)
        for g in range(H):
            normal = acc[g * half : (g + 1) * half, :] * scale[g * half : (g + 1) * half, :]
            pv_ref[part, g * half : (g + 1) * half, :] = normal.astype(BF16)
            out = out + normal * post_ref[g : g + 1, :]
        o_ref[part * half : (part + 1) * half, :] = out.astype(BF16)


def backward_kernel(n, sources, count, masks, half, rank_ref, q_ref, go_ref, lse_ref, pv_ref, pre_ref, post_ref, *rest):
    pieces = rest[:count]
    gq_ref, pre_grad_ref, post_grad_ref = rest[count : count + 3]
    grads = rest[count + 3 : count + 3 + n]
    kv, qg, gg, gk, gv, acc, sems, out_sems = rest[count + 3 + n :]
    rank = rank_ref[0]
    rows = H * half
    copies = load_keys(sources, n, half, rank, pieces, kv, sems)
    gk[...] = jnp.zeros(gk.shape, F32)
    gv[...] = jnp.zeros(gv.shape, F32)
    pre_grad_ref[...] = jnp.zeros(pre_grad_ref.shape, F32)
    post_grad_ref[...] = jnp.zeros(post_grad_ref.shape, F32)
    for copy in copies:
        copy.wait()
    for part in range(2):
        place = rank if part == 0 else 2 * n - 1 - rank
        live = (place * half + half + CHUNK - 1) // CHUNK
        q_part = q_ref[part * half : (part + 1) * half, :].astype(F32)
        go_part = go_ref[part * half : (part + 1) * half, :].astype(F32)
        row_dots = []
        for g in range(H):
            qg[g * half : (g + 1) * half, :] = (q_part * pre_ref[g : g + 1, :]).astype(BF16)
            mixed = go_part * post_ref[g : g + 1, :]
            gg[g * half : (g + 1) * half, :] = mixed.astype(BF16)
            normal = pv_ref[part, g * half : (g + 1) * half, :].astype(F32)
            row_dots.append(jnp.sum(mixed * normal, axis=1, keepdims=True))
            post_grad_ref[g : g + 1, :] += jnp.sum(go_part * normal, axis=0, keepdims=True)
        row_dot = jnp.broadcast_to(jnp.concatenate(row_dots, axis=0), (rows, 128))
        row_dot = jnp.transpose(row_dot)[:1, :]
        lse = lse_ref[part][:1, :]
        acc[...] = jnp.zeros((rows, D), F32)
        spot = place * half + lax.broadcasted_iota(jnp.int32, (CHUNK, rows), 1) % half
        line = lax.broadcasted_iota(jnp.int32, (CHUNK, rows), 0)

        def block(c, carry):
            start = pl.multiple_of(c * CHUNK, CHUNK)
            keys = kv[pl.ds(start, CHUNK), :D]
            values = kv[pl.ds(start, CHUNK), D:]
            found = dot(keys, qg[...], ((1,), (1,)))
            found = jnp.where(start + line <= spot, found, NEGATIVE)
            prob = jnp.exp(found - lse)
            grad_prob = dot(values, gg[...], ((1,), (1,)))
            grad_logit = (prob * (grad_prob - row_dot)).astype(BF16)
            gv[pl.ds(start, CHUNK), :] += dot(prob.astype(BF16), gg[...], ((1,), (0,)))
            gk[pl.ds(start, CHUNK), :] += dot(grad_logit, qg[...], ((1,), (0,)))
            acc[...] += dot(grad_logit, keys, ((0,), (0,)))
            return carry

        lax.fori_loop(0, live, block, 0)
        gq = jnp.zeros((half, D), F32)
        for g in range(H):
            found = acc[g * half : (g + 1) * half, :]
            gq = gq + found * pre_ref[g : g + 1, :]
            pre_grad_ref[g : g + 1, :] += jnp.sum(found * q_part, axis=0, keepdims=True)
        gq_ref[part * half : (part + 1) * half, :] = gq.astype(BF16)
    kv[:, :D] = gk[...].astype(BF16)
    kv[:, D:] = gv[...].astype(BF16)
    copies = []
    for index, mask in enumerate(masks):
        owner = rank ^ mask
        for part, place in ((0, owner), (1, 2 * n - 1 - owner)):
            start = pl.multiple_of(place * half, half)
            copies.append(
                pltpu.make_async_copy(
                    kv.at[pl.ds(start, half)],
                    grads[index].at[pl.ds(part * half, half)],
                    out_sems.at[2 * index + part],
                )
            )
    for copy in copies:
        copy.start()
    for copy in copies:
        copy.wait()


VMEM = pl.BlockSpec(memory_space=pltpu.VMEM)
SMEM = pl.BlockSpec(memory_space=pltpu.SMEM)
ANY = pl.BlockSpec(memory_space=pl.ANY)
LIMIT = pltpu.CompilerParams(vmem_limit_bytes=58 * 2**20)


def attend(n, sources, rank, queries, pieces, pre, post):
    count = len(pieces)
    tokens = queries.shape[0]
    half = tokens // 2
    rows = H * half
    length = n * tokens
    return pl.pallas_call(
        functools.partial(forward_kernel, n, sources, count, half),
        out_shape=(
            jax.ShapeDtypeStruct((tokens, D), BF16),
            jax.ShapeDtypeStruct((2, 8, rows), F32),
            jax.ShapeDtypeStruct((2, rows, D), BF16),
        ),
        in_specs=[SMEM, VMEM, VMEM, VMEM] + [ANY] * count,
        out_specs=(VMEM, VMEM, VMEM),
        scratch_shapes=[
            pltpu.VMEM((length, 2 * D), BF16),
            pltpu.VMEM((rows, D), BF16),
            pltpu.VMEM((length // CHUNK, rows, CHUNK), F32),
            pltpu.VMEM((rows, 128), F32),
            pltpu.VMEM((rows, 128), F32),
            pltpu.VMEM((rows, D), F32),
            pltpu.SemaphoreType.DMA((2 * n,)),
        ],
        compiler_params=LIMIT,
        cost_estimate=pl.CostEstimate(flops=10**10, bytes_accessed=8 * 2**20, transcendentals=2**20),
        name="attend",
    )(rank, queries, pre, post, *pieces)


def attend_back(sources, masks, rank, queries, grad_out, lse, pv, pieces, pre, post):
    n = len(masks)
    count = len(pieces)
    tokens = queries.shape[0]
    half = tokens // 2
    rows = H * half
    length = n * tokens
    outs = pl.pallas_call(
        functools.partial(backward_kernel, n, sources, count, masks, half),
        out_shape=(
            jax.ShapeDtypeStruct((tokens, D), BF16),
            jax.ShapeDtypeStruct((H, D), F32),
            jax.ShapeDtypeStruct((H, D), F32),
        )
        + tuple(jax.ShapeDtypeStruct((tokens, 2 * D), BF16) for _ in masks),
        in_specs=[SMEM] + [VMEM] * 6 + [ANY] * count,
        out_specs=(VMEM, VMEM, VMEM) + (ANY,) * n,
        scratch_shapes=[
            pltpu.VMEM((length, 2 * D), BF16),
            pltpu.VMEM((rows, D), BF16),
            pltpu.VMEM((rows, D), BF16),
            pltpu.VMEM((length, D), F32),
            pltpu.VMEM((length, D), F32),
            pltpu.VMEM((rows, D), F32),
            pltpu.SemaphoreType.DMA((2 * n,)),
            pltpu.SemaphoreType.DMA((2 * n,)),
        ],
        compiler_params=LIMIT,
        cost_estimate=pl.CostEstimate(flops=16 * 10**9, bytes_accessed=12 * 2**20, transcendentals=2**20),
        name="attend_back",
    )(rank, queries, grad_out, lse, pv, pre, post, *pieces)
    return outs[0], outs[1], outs[2], outs[3:]


def mm(a, b):
    return jnp.dot(a, b, preferred_element_type=F32)


def mm_t(a, b):
    return lax.dot_general(a, b, (((1,), (1,)), ((), ())), preferred_element_type=F32)


def t_mm(a, b):
    return lax.dot_general(a, b, (((0,), (0,)), ((), ())), preferred_element_type=F32)


def norm_parts(x):
    return lax.rsqrt(jnp.mean(x * x, axis=-1, keepdims=True) + 1e-06)


def norm_back(x, gain, grad):
    r = norm_parts(x)
    gain_grad = jnp.sum(grad * x * r, axis=0)
    scaled = grad * gain
    x_grad = r * scaled - x * (r * r * r) * jnp.mean(scaled * x, axis=-1, keepdims=True)
    return x_grad, gain_grad


def shards(
    geo,
    token_ids,
    embedding,
    gain_attn,
    w_qkv,
    w_proj,
    gain_ffn,
    w_in,
    w_back,
    mix_pre,
    mix_post,
    cotangent,
):
    n, r, count, core = geo.n, geo.r, geo.count, geo.core
    tokens = token_ids.size
    half = tokens // 2
    i = lax.axis_index("batch")
    j = lax.axis_index("seq")
    me = i * n + j
    rank = i * r + j % r
    rank_arg = rank.reshape(1).astype(jnp.int32)
    share = w_qkv.shape[1]
    back_share = w_back.shape[1]
    folds = back_share // share
    ff = w_in.shape[2]
    sw = functools.partial(swap, count=count)

    def packed_in(l):
        return w_in[l].reshape(share, count, folds, share).transpose(0, 2, 1, 3).reshape(share, ff)

    def packed_back(l):
        return jnp.concatenate([w_back[l, a * share : (a + 1) * share] for a in range(folds)], axis=1)

    gains = jnp.stack([gain_attn[0], gain_ffn[0], gain_attn[1], gain_ffn[1]], axis=1)
    gains = jnp.pad(gains, ((0, 0), (0, 124)))
    wide = [w_qkv[0], w_proj[0], gains]
    pairs = [
        jnp.concatenate(wide + [packed_in(0), packed_back(0)][:1], axis=1),
        jnp.concatenate([packed_back(0), w_qkv[1], w_proj[1]], axis=1),
        jnp.concatenate([packed_in(1), packed_back(1)], axis=1),
    ]
    borders = [4 * D + gains.shape[1], folds * D, ff]
    routes = [geo.x_last, geo.y_last]
    shared = len(geo.zs).bit_length() - 1
    stages = len(geo.x_last) - 1
    timed = stages == 4
    split = [None] * len(pairs)
    last_round = [None]

    def begin_round(number, after, late=()):
        pending = []
        for p in range(len(pairs)):
            k = number - 2 * p
            if 0 <= k < shared:
                pending.append((p, None, geo.x_last[k], pairs[p]))
            elif shared <= k < stages:
                if k == shared:
                    split[p] = [pairs[p][:, : borders[p]], pairs[p][:, borders[p] :]]
                pending += [(p, side, routes[side][k], split[p][side]) for side in range(2)]
        values = [entry[3] for entry in pending]
        if timed:
            values = list(lax.optimization_barrier((values, after, last_round[0]))[0])
            for index, wait in late:
                values[index], _ = lax.optimization_barrier((values[index], wait))
        arrived = [sw(value, entry[2]) for value, entry in zip(values, pending)]
        last_round[0] = arrived
        return pending, values, arrived

    def end_round(state, hold):
        pending, values, arrived = state
        if timed and hold is not None:
            arrived = lax.optimization_barrier((arrived, hold))[0]
            last_round[0] = arrived
        for value, there, (p, side, _, _) in zip(values, arrived, pending):
            joined = jnp.concatenate([value, there], axis=0)
            if side is None:
                pairs[p] = joined
            else:
                split[p][side] = joined

    ids_route = [geo.x_last[-2]] + [m for m in geo.x_last[:-2]] + [core]
    ids = token_ids.reshape(1, tokens)
    ids_stages = []
    for mask in ids_route:
        ids = jnp.concatenate([ids, sw(ids, mask)], axis=0)
        ids_stages.append(ids)
    first_ids, deep_ids = ids_stages[0], ids_stages[len(geo.zs).bit_length() - 1]
    target = me ^ jnp.array(geo.order, jnp.int32)
    t_seq = (target % n) // r
    t_rank = (target // n) * r + target % r
    halves = jnp.stack([t_rank, 2 * n - 1 - t_rank], axis=1)
    source = (t_seq[:, None] * n + halves // 2) ^ me
    source = sum(((source // mask) % 2) * 2**k for k, mask in enumerate(ids_route))
    ids = jnp.take(ids.reshape(2 * count, half), (source * 2 + halves % 2).reshape(-1), axis=0).reshape(-1)

    vocab = embedding.shape[0]
    line = jnp.arange(vocab, dtype=jnp.int32)
    table, first_ids = lax.optimization_barrier((embedding, first_ids))
    tables = [table] + [sw(table, m) for m in geo.high[1:]]
    tables = tables + [sw(part, core) for part in tables]
    owners = geo.high + [m ^ core for m in geo.high]
    end_round(begin_round(0, deep_ids), None)
    end_round(begin_round(1, deep_ids), None)
    third = begin_round(2, deep_ids)
    near = ids[: len(geo.low) * len(geo.zs) * tokens]
    picked = jnp.zeros((near.shape[0], D), F32)
    for m, part in zip(owners, tables):
        picked = picked + mm((near[:, None] == ((me ^ m) * vocab + line)[None, :]).astype(BF16), part)
    picked = picked.astype(BF16)
    end_round(third, picked)
    flat = picked.reshape(len(geo.low), -1, D)
    row = flat[0]
    for k in range(1, len(geo.low)):
        row = row + sw(flat[k], geo.low[k])
    fourth = begin_round(3, picked, [(1, row), (2, row)])
    row = row.reshape(len(geo.zs), tokens, D)
    stream = row[0]
    for k in range(1, len(geo.zs)):
        stream = stream + sw(row[k], geo.zs[k])
    stream = stream.astype(F32)
    end_round(fourth, stream)
    fifth = begin_round(4, stream)
    if not timed:
        end_round(fifth, None)
        for number in range(5, stages + 2 * len(pairs) - 2):
            end_round(begin_round(number, None), None)

    side = D // 2
    feature = jnp.arange(D, dtype=jnp.int32)

    def turner(route):
        order = jnp.repeat(jnp.array(reached(route), jnp.int32), share)
        origin = (me ^ order) * share + feature % share
        return (feature[:, None] == origin[None, :]).astype(BF16)

    turn_x, turn_y = turner(geo.x_last), turner(geo.y_last)

    def relative(value, turn):
        turned = mm(value, turn).astype(BF16)
        return turned[:, :side], turned[:, side:]

    def times(value, pair, start, width):
        near, far = pair
        return mm(value[0], near[:, start : start + width]) + mm(value[1], far[:, start : start + width])

    def back_times(value, pair, start, width, turn):
        near, far = pair
        near, far = (mm_t(value, side[:, start : start + width]).astype(BF16) for side in (near, far))
        return mm_t(jnp.concatenate([near, far], axis=1), turn)

    def finish(p):
        return [(value, sw(value, core)) for value in split[p]]

    turns = [turn_x, turn_y]
    attns, inwards, outwards = [None] * LAYERS, [None] * LAYERS, [None] * LAYERS
    attns[0], inwards[0] = finish(0)
    gain_all = jnp.concatenate([side[:, 4 * D : 4 * D + 8] for side in attns[0]], axis=0)
    gain_all = mm(turn_x, gain_all).T

    class Sum:
        def __init__(self, value, route):
            self.value = value
            self.masks = list(route[:-2])

        def outgoing(self):
            if not self.masks:
                return []
            return [(self.value[self.value.shape[0] // 2 :], self.masks.pop())]

        def incoming(self, arrived):
            for there in arrived:
                rows = self.value.shape[0] // 2
                self.value = self.value[:rows].astype(F32) + there.astype(F32)
                if self.masks:
                    self.value = self.value.astype(BF16)

        def step(self):
            self.incoming([sw(value, mask) for value, mask in self.outgoing()])

        def result(self):
            while self.masks:
                self.step()
            return self.value

    def exchange(after, sums, others=()):
        entries = list(others)
        spans = []
        for one in sums:
            out = one.outgoing()
            spans.append(len(out))
            entries += out
        values = lax.optimization_barrier(([value for value, _ in entries], after))[0]
        arrived = [sw(value, mask) for value, (_, mask) in zip(values, entries)]
        arrived = list(lax.optimization_barrier(arrived))
        place = len(others)
        for one, span in zip(sums, spans):
            one.incoming(arrived[place : place + span])
            place += span
        return arrived[: len(others)]

    def tie(value, sums):
        value, held_sums = lax.optimization_barrier((value, [one.value for one in sums]))
        for one, held_sum in zip(sums, held_sums):
            one.value = held_sum
        return value

    x_mask = geo.x_last[-2]
    quarter = D // 4
    quarters = [turn_x[:, k * quarter : (k + 1) * quarter] for k in range(4)]

    def four_rows(values, quarters):
        tall = jnp.concatenate(values, axis=0)
        stay, to_x, to_core, to_both = (mm(tall, q).astype(BF16) for q in quarters)
        size = tall.shape[0]
        from_x = sw(jnp.concatenate([to_x, to_both], axis=0), x_mask)
        rest = sw(jnp.concatenate([to_core, from_x[size:]], axis=0), core)
        spots = [slice(k * tokens, (k + 1) * tokens) for k in range(len(values))]
        return [
            jnp.concatenate([stay[s], from_x[:size][s], rest[:size][s], rest[size:][s]], axis=0) for s in spots
        ]

    def two_tokens(value):
        return jnp.concatenate([value, sw(value, x_mask)], axis=0)

    def four_tokens(value):
        return jnp.concatenate([value, sw(value, core)], axis=0)

    def side_by_side(parts):
        return jnp.concatenate([part.astype(BF16) for part in parts], axis=1)

    def fold(value, a):
        return tuple(side[a * tokens : (a + 1) * tokens] for side in value)

    def half_moves(parity):
        moves = []
        for b in range(geo.b):
            for block in range(n):
                h = 2 * block + parity
                to = geo.device(b, h if h < n else 2 * n - 1 - h)
                moves.append((b * n + block, to))
        return moves

    flat, _ = lax.optimization_barrier((cotangent.reshape(tokens, D), stream))
    evens = lax.ppermute(flat[:half], AXES, half_moves(0))
    odds = lax.ppermute(flat[half:], AXES, half_moves(1))
    even_rank = rank % 2 == 0
    grad_stream = jnp.where(
        even_rank, jnp.concatenate([evens, odds], axis=0), jnp.concatenate([odds, evens], axis=0)
    ).astype(F32)

    near_masks = list(geo.plane)
    masks = [geo.rank_mask(m) for m in near_masks] + [geo.rank_mask(m ^ core) for m in near_masks]
    if len(near_masks) == 4:
        near_sources = [(k, part * half, m, part) for k, m in enumerate(masks[:3]) for part in range(2)]
        near_sources += [(3, 0, masks[3], 0), (4, 0, masks[3], 1)]
    else:
        near_sources = [(k, part * half, m, part) for k, m in enumerate(masks[:n // 2]) for part in range(2)]
    piece_count = near_sources[-1][0] + 1
    sources = near_sources + [
        (k + piece_count, row, m ^ geo.rank_mask(core), part) for k, row, m, part in near_sources
    ]

    spread_pre = [jnp.repeat(mix_pre[l].T, E, axis=1) * E ** (-0.5) for l in range(LAYERS)]
    spread_post = [jnp.repeat(mix_post[l], E, axis=1) for l in range(LAYERS)]

    def spread_keys(own):
        if len(near_masks) == 4:
            y, x = near_masks[1], near_masks[2]
            by_y, by_x = sw(own, y), sw(own, x)
            return [own, by_y, by_x, sw(by_x[:half], y), sw(by_y[half:], x)]
        return [own] + [sw(own, m) for m in near_masks[1:]]

    saved = []
    for l in range(LAYERS):
        gain_a, gain_f = gain_all[2 * l], gain_all[2 * l + 1]
        turn = turns[l]
        n1 = (stream * norm_parts(stream) * gain_a).astype(BF16)
        projected = times(relative(n1, turn), attns[l], 0, 3 * D).astype(BF16)
        queries = projected[:, :D]
        if timed and l == 0:
            end_round(fifth, projected)
            sixth = begin_round(5, projected)
        pieces = spread_keys(projected[:, D:])
        pieces = pieces + [sw(piece, core) for piece in pieces]
        attended, lse, pv = attend(n, sources, rank_arg, queries, pieces, spread_pre[l], spread_post[l])
        if timed:
            end_round(sixth if l == 0 else eighth, attended)
        if l == 0:
            if timed:
                seventh = begin_round(6, attended)
            outwards[0], attns[1] = finish(1)
        else:
            inwards[1], outwards[1] = finish(2)
        middle = stream + times(relative(attended, turn), attns[l], 3 * D, D)
        n2 = (middle * norm_parts(middle) * gain_f).astype(BF16)
        hidden = times(relative(n2, turns[1 - l]), inwards[l], 0, ff)
        active = jax.nn.gelu(hidden, approximate=True).astype(BF16)
        wide = relative(jnp.concatenate([active[:, a * D : (a + 1) * D] for a in range(folds)], axis=0), turns[l])
        stream_in, stream = stream, middle
        for a in range(folds):
            stream = stream + times(fold(wide, a), outwards[l], a * D, D)
        if timed and l == 0:
            end_round(seventh, stream)
            eighth = begin_round(7, stream)
        saved.append((stream_in, n1, queries, pieces, attended, lse, pv, middle, n2, hidden, active, wide))

    final = stream.astype(BF16)
    back_even = [(b, a) for a, b in half_moves(0)]
    back_odd = [(b, a) for a, b in half_moves(1)]
    first = jnp.where(even_rank, final[:half], final[half:])
    second = jnp.where(even_rank, final[half:], final[:half])
    output = [lax.ppermute(first, AXES, back_even), lax.ppermute(second, AXES, back_odd)]

    mixes = [None] * LAYERS
    gain_grads = [None] * LAYERS
    for l in reversed(range(LAYERS)):
        gain_a, gain_f = gain_all[2 * l], gain_all[2 * l + 1]
        stream_in, n1, queries, pieces, attended, lse, pv, middle, n2, hidden, active, wide = saved[l]
        gf = grad_stream.astype(BF16)
        pull = jax.vjp(lambda z: jax.nn.gelu(z, approximate=True), hidden)[1]
        active_grad = [back_times(gf, outwards[l], a * D, D, turns[l]) for a in range(folds)]
        gz = pull(jnp.concatenate(active_grad, axis=1))[0].astype(BF16)
        normed_grad = back_times(gz, inwards[l], 0, ff, turns[1 - l])
        by_fold = [active[:, a * D : (a + 1) * D] for a in range(folds)]
        gf_two = two_tokens(gf)
        if l == 0:
            tall = four_rows(by_fold, quarters)
            tall_n2, tall_out, tall_n1 = four_rows([n2, attended, n1], quarters)
        else:
            gz_two = two_tokens(gz)
            tall = four_rows([n2] + by_fold, quarters)
        delta, gain_f_grad = norm_back(middle, gain_f, normed_grad)
        middle_grad = grad_stream + delta
        gy = middle_grad.astype(BF16)
        go = back_times(gy, attns[l], 3 * D, D, turns[l]).astype(BF16)
        if l == 0:
            gz_two = two_tokens(jnp.concatenate([gz, gy], axis=1))
            go, gf_two = lax.optimization_barrier((go, gf_two))
            gf_four = four_tokens(gf_two)
            back_sum = Sum(side_by_side([t_mm(part, gf_four) for part in tall]), geo.x_last)
            back_sum.step()
            ffn_sum.step()
        gq, pre_grad, post_grad, parts = attend_back(
            sources, masks, rank_arg, queries, go, lse, pv, pieces, spread_pre[l], spread_post[l]
        )
        mixes[l] = (pre_grad, post_grad)
        if l == 1:
            parts, output = lax.optimization_barrier((parts, output))
        if l == 0:
            parts, gz_two, both_two = lax.optimization_barrier((parts, gz_two, both_two))
            parts = tie(parts, [back_sum, ffn_sum])
        size = len(near_masks)
        sums = [parts[k].astype(F32) + sw(parts[size + k], core).astype(F32) for k in range(size)]
        others = [(sums[k].astype(BF16), near_masks[k]) for k in range(1, size)]
        if l == 0:
            arrived = exchange(parts[0], [ffn_sum], others)
            gz_two, both_two, _ = lax.optimization_barrier((gz_two, both_two, sums))
            gz_four, both = four_tokens(gz_two), four_tokens(both_two)
            attn_grad = [t_mm(tall_n1_one, both[:, : 3 * D]), t_mm(tall_out_one, both[:, 3 * D :])]
            in_grad = [t_mm(tall_n2, gz_four[:, :ff]), t_mm(tall_out, gz_four[:, ff:])]
            joined_sum = Sum(side_by_side(attn_grad + in_grad), geo.x_last)
            arrived = tie(arrived, [joined_sum])
        else:
            arrived = [sw(value, mask) for value, mask in others]
            gz_two, gf_two, _ = lax.optimization_barrier((gz_two, gf_two, sums))
            gz_four, gf_four = four_tokens(gz_two), four_tokens(gf_two)
            ffn_grad = [t_mm(tall[0], gz_four)] + [t_mm(part, gf_four) for part in tall[1:]]
            ffn_sum = Sum(side_by_side(ffn_grad), geo.x_last)
            arrived = tie(arrived, [ffn_sum])
        kv_grad = sums[0]
        for there in arrived:
            kv_grad = kv_grad + there.astype(F32)
        joint = jnp.concatenate([gq, kv_grad.astype(BF16)], axis=1)
        normed_grad = back_times(joint, attns[l], 0, 3 * D, turns[l])
        if l == 0:
            joint_zero = joint
        else:
            both_two = two_tokens(jnp.concatenate([joint, gy], axis=1))
            tall_n1_one, tall_out_one = four_rows([n1, attended], quarters)
        delta, gain_a_grad = norm_back(stream_in, gain_a, normed_grad)
        grad_stream = middle_grad + delta
        gain_grads[l] = (gain_a_grad, gain_f_grad)

    pre_sum = jnp.stack([mixes[l][0] for l in range(LAYERS)]).reshape(LAYERS, H, H, E).sum(-1)
    post_sum = jnp.stack([mixes[l][1] for l in range(LAYERS)]).reshape(LAYERS, H, H, E).sum(-1)
    small = jnp.concatenate(
        [(pre_sum.transpose(0, 2, 1) * E ** (-0.5)).reshape(-1), post_sum.reshape(-1)]
        + [gain_grads[l][k] for k in range(2) for l in range(LAYERS)]
    )
    size = small.shape[0]
    small = jnp.pad(small, (0, -size % 1024)).reshape(-1, 128)
    small_masks = bits(1, count)

    g0 = grad_stream.astype(BF16)
    arrived = exchange(g0, [joined_sum], [(joint_zero, x_mask)] + [(g0, m) for m in geo.zs[1:]])
    joint_four = four_tokens(jnp.concatenate([joint_zero, arrived[0]], axis=0))
    qkv_sum = Sum(t_mm(tall_n1, joint_four).astype(BF16), geo.x_last)
    rows = jnp.concatenate([g0] + arrived[1:], axis=0)

    def share_small(after, sums, others=()):
        nonlocal small
        there = exchange(after, sums, list(others) + [(small, small_masks.pop())])
        small = small + there[-1]
        return there[:-1]

    if len(geo.plane) == 4:
        cut = rows.shape[0] // 2
        y, x = geo.plane[1], geo.plane[2]
        by_y, by_x = share_small(rows, [joined_sum, back_sum], [(rows, y), (rows, x)])
        both = share_small(by_x, [qkv_sum, joined_sum], [(by_x[:cut], y), (by_y[cut:], x)])
        blocks = [rows, by_y, by_x] + both
    else:
        blocks = [rows] + share_small(rows, [joined_sum, back_sum], [(rows, m) for m in geo.plane[1:]])
        share_small(blocks[-1], [qkv_sum, joined_sum])
    blocks = blocks + [sw(block, core) for block in blocks]
    share_small(blocks, [qkv_sum, back_sum, ffn_sum])
    own_names = me * vocab + line
    blocks = jnp.concatenate(blocks, axis=0)
    embedding_grad = mm(
        (own_names[:, None] == ids[None, :]).astype(BF16), blocks
    )
    while len(small_masks) > 2:
        share_small(qkv_sum.value, [qkv_sum])
    one_bit, two_bit = small_masks
    one, two, both = exchange(qkv_sum.value, [qkv_sum], [(small, one_bit), (small, two_bit), (small, one_bit ^ two_bit)])
    small = (small + one) + (two + both)
    small = small.reshape(-1)[:size]
    mix = small[: 2 * LAYERS * H * H].reshape(2, LAYERS, H, H)
    gain_sum = small[2 * LAYERS * H * H :].reshape(2, LAYERS, D)
    gain_sum = lax.dynamic_slice(gain_sum, (0, 0, me * share), (2, LAYERS, share))

    def in_order(part):
        return part.reshape(share, folds, count, share).transpose(0, 2, 1, 3).reshape(share, ff)

    def back_order(part):
        return jnp.concatenate([part[:, a * D : (a + 1) * D] for a in range(folds)], axis=0)

    qkv_share = qkv_sum.result()
    one, joined, zero = ffn_sum.result(), joined_sum.result(), back_sum.result()
    attn_share, in_share = joined[:, : 4 * D], joined[:, 4 * D :]
    output = jnp.concatenate(output, axis=0).reshape(cotangent.shape)
    return (
        output,
        embedding_grad,
        gain_sum[0],
        jnp.stack([qkv_share, attn_share[:, : 3 * D]]),
        jnp.stack([in_share[:, ff:], attn_share[:, 3 * D :]]),
        gain_sum[1],
        jnp.stack([in_order(in_share[:, :ff]), in_order(one[:, :ff])]),
        jnp.stack([back_order(zero), back_order(one[:, ff:])]),
        mix[0],
        mix[1],
    )


def solution(mesh):
    everywhere = ("batch", "seq")
    weight = P(None, everywhere, None)
    vector = P(None, everywhere)
    return jax.shard_map(
        functools.partial(shards, Geometry(mesh)),
        mesh=mesh,
        in_specs=(
            P("batch", "seq"),
            P(everywhere, None),
            vector,
            weight,
            weight,
            vector,
            weight,
            weight,
            P(),
            P(),
            P("batch", "seq", None),
        ),
        out_specs=(
            P("batch", "seq", None),
            P(everywhere, None),
            vector,
            weight,
            weight,
            vector,
            weight,
            weight,
            P(),
            P(),
        ),
        check_vma=False,
    )
```

```python
import functools

import jax
import jax.numpy as jnp
from jax import lax
from jax.experimental import pallas as pl
from jax.experimental.pallas import tpu as pltpu
from jax.sharding import PartitionSpec as P

D = 768
H = 12
E = 64
LAYERS = 2
AXES = ("batch", "seq")
NEGATIVE = -1e30
CHUNK = 256
F32 = jnp.float32
BF16 = jnp.bfloat16


class Geometry:
    def __init__(self, mesh):
        self.b = mesh.shape["batch"]
        self.n = mesh.shape["seq"]
        self.r = self.n // self.b
        self.count = self.b * self.n
        self.core = self.n
        low = list(range(self.r))
        self.high = [k * self.n for k in range(0, self.b, 2)]
        self.low = low
        self.plane = [h + l for h in self.high for l in low]
        self.zs = [k * self.r for k in range(self.b)]
        self.order = [c + h + l + z for c in (0, self.core) for h in self.high for l in low for z in self.zs]
        z_bits = bits(self.r, self.n)[::-1]
        x_bits = [bit for bit in bits(self.n, self.count) if bit != self.core]
        y_bits = bits(1, self.r)
        self.x_last = z_bits + y_bits + x_bits + [self.core]
        self.y_last = z_bits + x_bits + y_bits + [self.core]

    def rank_mask(self, mask):
        return (mask // self.n) * self.r + mask % self.n

    def device(self, sequence, rank):
        return (rank // self.r) * self.n + sequence * self.r + rank % self.r


def bits(first, end):
    found = []
    while first < end:
        found.append(first)
        first *= 2
    return found


def reached(masks):
    order = [0]
    for mask in masks:
        order = order + [o ^ mask for o in order]
    return order


def swap(value, mask, count):
    return lax.ppermute(value, AXES, [(p, p ^ mask) for p in range(count)])


def dot(a, b, contract):
    return lax.dot_general(a, b, (contract, ((), ())), preferred_element_type=F32)


def load_keys(sources, n, half, rank, pieces, kv, sems):
    copies = []
    for k, (index, row, mask, part) in enumerate(sources):
        owner = rank ^ mask
        place = owner if part == 0 else 2 * n - 1 - owner
        copies.append(
            pltpu.make_async_copy(
                pieces[index].at[pl.ds(row, half)],
                kv.at[pl.ds(pl.multiple_of(place * half, half), half)],
                sems.at[k],
            )
        )
    for copy in copies:
        copy.start()
    return copies


def mixed_rows(rows, weights):
    return jnp.concatenate([rows * weights[g : g + 1, :] for g in range(H)], axis=0)


def forward_kernel(n, sources, count, half, rank_ref, q_ref, pre_ref, post_ref, *rest):
    pieces = rest[:count]
    o_ref, lse_ref, pv_ref = rest[count : count + 3]
    kv, qg, logits, top, total, acc, sems = rest[count + 3 :]
    rank = rank_ref[0]
    rows = H * half
    copies = load_keys(sources, n, half, rank, pieces, kv, sems)
    for copy in copies:
        copy.wait()
    for part in range(2):
        place = rank if part == 0 else 2 * n - 1 - rank
        live = (place * half + half + CHUNK - 1) // CHUNK
        q_part = q_ref[part * half : (part + 1) * half, :].astype(F32)
        qg[...] = mixed_rows(q_part, pre_ref[...]).astype(BF16)
        top[...] = jnp.full((rows, 128), NEGATIVE, F32)
        total[...] = jnp.zeros((rows, 128), F32)
        acc[...] = jnp.zeros((rows, D), F32)
        spot = place * half + lax.broadcasted_iota(jnp.int32, (rows, CHUNK), 0) % half
        lane = lax.broadcasted_iota(jnp.int32, (rows, CHUNK), 1)

        def score(c, carry):
            start = pl.multiple_of(c * CHUNK, CHUNK)
            found = dot(qg[...], kv[pl.ds(start, CHUNK), :D], ((1,), (1,)))
            found = jnp.where(start + lane <= spot, found, NEGATIVE)
            logits[c] = found
            best = found[:, :128]
            for k in range(1, CHUNK // 128):
                best = jnp.maximum(best, found[:, k * 128 : (k + 1) * 128])
            top[...] = jnp.maximum(top[...], best)
            return carry

        lax.fori_loop(0, live, score, 0)
        row_max = jnp.max(top[...], axis=1, keepdims=True)

        def weigh(c, carry):
            start = pl.multiple_of(c * CHUNK, CHUNK)
            prob = jnp.exp(logits[c] - row_max)
            part_sum = prob[:, :128]
            for k in range(1, CHUNK // 128):
                part_sum = part_sum + prob[:, k * 128 : (k + 1) * 128]
            total[...] += part_sum
            acc[...] += dot(prob.astype(BF16), kv[pl.ds(start, CHUNK), D:], ((1,), (0,)))
            return carry

        lax.fori_loop(0, live, weigh, 0)
        row_sum = jnp.sum(total[...], axis=1, keepdims=True)
        scale = 1.0 / row_sum
        lse = jnp.broadcast_to(row_max + jnp.log(row_sum), (rows, 128))
        lse_ref[part] = jnp.transpose(lse)[:8, :]
        out = jnp.zeros((half, D), F32)
        for g in range(H):
            normal = acc[g * half : (g + 1) * half, :] * scale[g * half : (g + 1) * half, :]
            pv_ref[part, g * half : (g + 1) * half, :] = normal.astype(BF16)
            out = out + normal * post_ref[g : g + 1, :]
        o_ref[part * half : (part + 1) * half, :] = out.astype(BF16)


def backward_kernel(n, sources, count, masks, half, rank_ref, q_ref, go_ref, lse_ref, pv_ref, pre_ref, post_ref, *rest):
    pieces = rest[:count]
    gq_ref, pre_grad_ref, post_grad_ref = rest[count : count + 3]
    grads = rest[count + 3 : count + 3 + n]
    kv, qg, gg, gk, gv, acc, sems, out_sems = rest[count + 3 + n :]
    rank = rank_ref[0]
    rows = H * half
    copies = load_keys(sources, n, half, rank, pieces, kv, sems)
    gk[...] = jnp.zeros(gk.shape, F32)
    gv[...] = jnp.zeros(gv.shape, F32)
    pre_grad_ref[...] = jnp.zeros(pre_grad_ref.shape, F32)
    post_grad_ref[...] = jnp.zeros(post_grad_ref.shape, F32)
    for copy in copies:
        copy.wait()
    for part in range(2):
        place = rank if part == 0 else 2 * n - 1 - rank
        live = (place * half + half + CHUNK - 1) // CHUNK
        q_part = q_ref[part * half : (part + 1) * half, :].astype(F32)
        go_part = go_ref[part * half : (part + 1) * half, :].astype(F32)
        row_dots = []
        for g in range(H):
            qg[g * half : (g + 1) * half, :] = (q_part * pre_ref[g : g + 1, :]).astype(BF16)
            mixed = go_part * post_ref[g : g + 1, :]
            gg[g * half : (g + 1) * half, :] = mixed.astype(BF16)
            normal = pv_ref[part, g * half : (g + 1) * half, :].astype(F32)
            row_dots.append(jnp.sum(mixed * normal, axis=1, keepdims=True))
            post_grad_ref[g : g + 1, :] += jnp.sum(go_part * normal, axis=0, keepdims=True)
        row_dot = jnp.broadcast_to(jnp.concatenate(row_dots, axis=0), (rows, 128))
        row_dot = jnp.transpose(row_dot)[:1, :]
        lse = lse_ref[part][:1, :]
        acc[...] = jnp.zeros((rows, D), F32)
        spot = place * half + lax.broadcasted_iota(jnp.int32, (CHUNK, rows), 1) % half
        line = lax.broadcasted_iota(jnp.int32, (CHUNK, rows), 0)

        def block(c, carry):
            start = pl.multiple_of(c * CHUNK, CHUNK)
            keys = kv[pl.ds(start, CHUNK), :D]
            values = kv[pl.ds(start, CHUNK), D:]
            found = dot(keys, qg[...], ((1,), (1,)))
            found = jnp.where(start + line <= spot, found, NEGATIVE)
            prob = jnp.exp(found - lse)
            grad_prob = dot(values, gg[...], ((1,), (1,)))
            grad_logit = (prob * (grad_prob - row_dot)).astype(BF16)
            gv[pl.ds(start, CHUNK), :] += dot(prob.astype(BF16), gg[...], ((1,), (0,)))
            gk[pl.ds(start, CHUNK), :] += dot(grad_logit, qg[...], ((1,), (0,)))
            acc[...] += dot(grad_logit, keys, ((0,), (0,)))
            return carry

        lax.fori_loop(0, live, block, 0)
        gq = jnp.zeros((half, D), F32)
        for g in range(H):
            found = acc[g * half : (g + 1) * half, :]
            gq = gq + found * pre_ref[g : g + 1, :]
            pre_grad_ref[g : g + 1, :] += jnp.sum(found * q_part, axis=0, keepdims=True)
        gq_ref[part * half : (part + 1) * half, :] = gq.astype(BF16)
    kv[:, :D] = gk[...].astype(BF16)
    kv[:, D:] = gv[...].astype(BF16)
    copies = []
    for index, mask in enumerate(masks):
        owner = rank ^ mask
        for part, place in ((0, owner), (1, 2 * n - 1 - owner)):
            start = pl.multiple_of(place * half, half)
            copies.append(
                pltpu.make_async_copy(
                    kv.at[pl.ds(start, half)],
                    grads[index].at[pl.ds(part * half, half)],
                    out_sems.at[2 * index + part],
                )
            )
    for copy in copies:
        copy.start()
    for copy in copies:
        copy.wait()


VMEM = pl.BlockSpec(memory_space=pltpu.VMEM)
SMEM = pl.BlockSpec(memory_space=pltpu.SMEM)
ANY = pl.BlockSpec(memory_space=pl.ANY)
LIMIT = pltpu.CompilerParams(vmem_limit_bytes=58 * 2**20)


def attend(n, sources, rank, queries, pieces, pre, post):
    count = len(pieces)
    tokens = queries.shape[0]
    half = tokens // 2
    rows = H * half
    length = n * tokens
    return pl.pallas_call(
        functools.partial(forward_kernel, n, sources, count, half),
        out_shape=(
            jax.ShapeDtypeStruct((tokens, D), BF16),
            jax.ShapeDtypeStruct((2, 8, rows), F32),
            jax.ShapeDtypeStruct((2, rows, D), BF16),
        ),
        in_specs=[SMEM, VMEM, VMEM, VMEM] + [ANY] * count,
        out_specs=(VMEM, VMEM, VMEM),
        scratch_shapes=[
            pltpu.VMEM((length, 2 * D), BF16),
            pltpu.VMEM((rows, D), BF16),
            pltpu.VMEM((length // CHUNK, rows, CHUNK), F32),
            pltpu.VMEM((rows, 128), F32),
            pltpu.VMEM((rows, 128), F32),
            pltpu.VMEM((rows, D), F32),
            pltpu.SemaphoreType.DMA((2 * n,)),
        ],
        compiler_params=LIMIT,
        cost_estimate=pl.CostEstimate(flops=10**8, bytes_accessed=8 * 2**20, transcendentals=2**20),
        name="attend",
    )(rank, queries, pre, post, *pieces)


def attend_back(sources, masks, rank, queries, grad_out, lse, pv, pieces, pre, post):
    n = len(masks)
    count = len(pieces)
    tokens = queries.shape[0]
    half = tokens // 2
    rows = H * half
    length = n * tokens
    outs = pl.pallas_call(
        functools.partial(backward_kernel, n, sources, count, masks, half),
        out_shape=(
            jax.ShapeDtypeStruct((tokens, D), BF16),
            jax.ShapeDtypeStruct((H, D), F32),
            jax.ShapeDtypeStruct((H, D), F32),
        )
        + tuple(jax.ShapeDtypeStruct((tokens, 2 * D), BF16) for _ in masks),
        in_specs=[SMEM] + [VMEM] * 6 + [ANY] * count,
        out_specs=(VMEM, VMEM, VMEM) + (ANY,) * n,
        scratch_shapes=[
            pltpu.VMEM((length, 2 * D), BF16),
            pltpu.VMEM((rows, D), BF16),
            pltpu.VMEM((rows, D), BF16),
            pltpu.VMEM((length, D), F32),
            pltpu.VMEM((length, D), F32),
            pltpu.VMEM((rows, D), F32),
            pltpu.SemaphoreType.DMA((2 * n,)),
            pltpu.SemaphoreType.DMA((2 * n,)),
        ],
        compiler_params=LIMIT,
        cost_estimate=pl.CostEstimate(flops=16 * 10**9, bytes_accessed=12 * 2**20, transcendentals=2**20),
        name="attend_back",
    )(rank, queries, grad_out, lse, pv, pre, post, *pieces)
    return outs[0], outs[1], outs[2], outs[3:]


def mm(a, b):
    return jnp.dot(a, b, preferred_element_type=F32)


def mm_t(a, b):
    return lax.dot_general(a, b, (((1,), (1,)), ((), ())), preferred_element_type=F32)


def t_mm(a, b):
    return lax.dot_general(a, b, (((0,), (0,)), ((), ())), preferred_element_type=F32)


def norm_parts(x):
    return lax.rsqrt(jnp.mean(x * x, axis=-1, keepdims=True) + 1e-06)


def norm_back(x, gain, grad):
    r = norm_parts(x)
    gain_grad = jnp.sum(grad * x * r, axis=0)
    scaled = grad * gain
    x_grad = r * scaled - x * (r * r * r) * jnp.mean(scaled * x, axis=-1, keepdims=True)
    return x_grad, gain_grad


def shards(
    geo,
    token_ids,
    embedding,
    gain_attn,
    w_qkv,
    w_proj,
    gain_ffn,
    w_in,
    w_back,
    mix_pre,
    mix_post,
    cotangent,
):
    n, r, count, core = geo.n, geo.r, geo.count, geo.core
    tokens = token_ids.size
    half = tokens // 2
    i = lax.axis_index("batch")
    j = lax.axis_index("seq")
    me = i * n + j
    rank = i * r + j % r
    rank_arg = rank.reshape(1).astype(jnp.int32)
    share = w_qkv.shape[1]
    back_share = w_back.shape[1]
    folds = back_share // share
    ff = w_in.shape[2]
    sw = functools.partial(swap, count=count)

    def packed_in(l):
        return w_in[l].reshape(share, count, folds, share).transpose(0, 2, 1, 3).reshape(share, ff)

    def packed_back(l):
        return jnp.concatenate([w_back[l, a * share : (a + 1) * share] for a in range(folds)], axis=1)

    gains = jnp.stack([gain_attn[0], gain_ffn[0], gain_attn[1], gain_ffn[1]], axis=1)
    gains = jnp.pad(gains, ((0, 0), (0, 124)))
    wide = [w_qkv[0], w_proj[0], gains]
    pairs = [
        jnp.concatenate(wide + [packed_in(0), packed_back(0)][:1], axis=1),
        jnp.concatenate([packed_back(0), w_qkv[1], w_proj[1]], axis=1),
        jnp.concatenate([packed_in(1), packed_back(1)], axis=1),
    ]
    borders = [4 * D + gains.shape[1], folds * D, ff]
    routes = [geo.x_last, geo.y_last]
    shared = len(geo.zs).bit_length() - 1
    stages = len(geo.x_last) - 1
    timed = stages == 4
    split = [None] * len(pairs)
    last_round = [None]

    def begin_round(number, after, late=()):
        pending = []
        for p in range(len(pairs)):
            k = number - 2 * p
            if 0 <= k < shared:
                pending.append((p, None, geo.x_last[k], pairs[p]))
            elif shared <= k < stages:
                if k == shared:
                    split[p] = [pairs[p][:, : borders[p]], pairs[p][:, borders[p] :]]
                pending += [(p, side, routes[side][k], split[p][side]) for side in range(2)]
        values = [entry[3] for entry in pending]
        if timed:
            values = list(lax.optimization_barrier((values, after, last_round[0]))[0])
            for index, wait in late:
                values[index], _ = lax.optimization_barrier((values[index], wait))
        arrived = [sw(value, entry[2]) for value, entry in zip(values, pending)]
        last_round[0] = arrived
        return pending, values, arrived

    def end_round(state, hold):
        pending, values, arrived = state
        if timed and hold is not None:
            arrived = lax.optimization_barrier((arrived, hold))[0]
            last_round[0] = arrived
        for value, there, (p, side, _, _) in zip(values, arrived, pending):
            joined = jnp.concatenate([value, there], axis=0)
            if side is None:
                pairs[p] = joined
            else:
                split[p][side] = joined

    ids_route = [geo.x_last[-2]] + [m for m in geo.x_last[:-2]] + [core]
    ids = token_ids.reshape(1, tokens)
    ids_stages = []
    for mask in ids_route:
        ids = jnp.concatenate([ids, sw(ids, mask)], axis=0)
        ids_stages.append(ids)
    first_ids, deep_ids = ids_stages[0], ids_stages[len(geo.zs).bit_length() - 1]
    target = me ^ jnp.array(geo.order, jnp.int32)
    t_seq = (target % n) // r
    t_rank = (target // n) * r + target % r
    halves = jnp.stack([t_rank, 2 * n - 1 - t_rank], axis=1)
    source = (t_seq[:, None] * n + halves // 2) ^ me
    source = sum(((source // mask) % 2) * 2**k for k, mask in enumerate(ids_route))
    ids = jnp.take(ids.reshape(2 * count, half), (source * 2 + halves % 2).reshape(-1), axis=0).reshape(-1)

    vocab = embedding.shape[0]
    line = jnp.arange(vocab, dtype=jnp.int32)
    table, first_ids = lax.optimization_barrier((embedding, first_ids))
    tables = [table] + [sw(table, m) for m in geo.high[1:]]
    tables = tables + [sw(part, core) for part in tables]
    owners = geo.high + [m ^ core for m in geo.high]
    end_round(begin_round(0, deep_ids), None)
    end_round(begin_round(1, deep_ids), None)
    third = begin_round(2, deep_ids)
    near = ids[: len(geo.low) * len(geo.zs) * tokens]
    picked = jnp.zeros((near.shape[0], D), F32)
    for m, part in zip(owners, tables):
        picked = picked + mm((near[:, None] == ((me ^ m) * vocab + line)[None, :]).astype(BF16), part)
    picked = picked.astype(BF16)
    end_round(third, picked)
    flat = picked.reshape(len(geo.low), -1, D)
    row = flat[0]
    for k in range(1, len(geo.low)):
        row = row + sw(flat[k], geo.low[k])
    fourth = begin_round(3, picked, [(1, row), (2, row)])
    row = row.reshape(len(geo.zs), tokens, D)
    stream = row[0]
    for k in range(1, len(geo.zs)):
        stream = stream + sw(row[k], geo.zs[k])
    stream = stream.astype(F32)
    end_round(fourth, stream)
    fifth = begin_round(4, stream)
    if not timed:
        end_round(fifth, None)
        for number in range(5, stages + 2 * len(pairs) - 2):
            end_round(begin_round(number, None), None)

    side = D // 2
    feature = jnp.arange(D, dtype=jnp.int32)

    def turner(route):
        order = jnp.repeat(jnp.array(reached(route), jnp.int32), share)
        origin = (me ^ order) * share + feature % share
        return (feature[:, None] == origin[None, :]).astype(BF16)

    turn_x, turn_y = turner(geo.x_last), turner(geo.y_last)

    def relative(value, turn):
        turned = mm(value, turn).astype(BF16)
        return turned[:, :side], turned[:, side:]

    def times(value, pair, start, width):
        near, far = pair
        return mm(value[0], near[:, start : start + width]) + mm(value[1], far[:, start : start + width])

    def back_times(value, pair, start, width, turn):
        near, far = pair
        near, far = (mm_t(value, side[:, start : start + width]).astype(BF16) for side in (near, far))
        return mm_t(jnp.concatenate([near, far], axis=1), turn)

    def finish(p):
        return [(value, sw(value, core)) for value in split[p]]

    turns = [turn_x, turn_y]
    attns, inwards, outwards = [None] * LAYERS, [None] * LAYERS, [None] * LAYERS
    attns[0], inwards[0] = finish(0)
    gain_all = jnp.concatenate([side[:, 4 * D : 4 * D + 8] for side in attns[0]], axis=0)
    gain_all = mm(turn_x, gain_all).T

    class Sum:
        def __init__(self, value, route):
            self.value = value
            self.masks = list(route[:-2])

        def outgoing(self):
            if not self.masks:
                return []
            return [(self.value[self.value.shape[0] // 2 :], self.masks.pop())]

        def incoming(self, arrived):
            for there in arrived:
                rows = self.value.shape[0] // 2
                self.value = self.value[:rows].astype(F32) + there.astype(F32)
                if self.masks:
                    self.value = self.value.astype(BF16)

        def step(self):
            self.incoming([sw(value, mask) for value, mask in self.outgoing()])

        def result(self):
            while self.masks:
                self.step()
            return self.value

    def exchange(after, sums, others=()):
        entries = list(others)
        spans = []
        for one in sums:
            out = one.outgoing()
            spans.append(len(out))
            entries += out
        values = lax.optimization_barrier(([value for value, _ in entries], after))[0]
        arrived = [sw(value, mask) for value, (_, mask) in zip(values, entries)]
        arrived = list(lax.optimization_barrier(arrived))
        place = len(others)
        for one, span in zip(sums, spans):
            one.incoming(arrived[place : place + span])
            place += span
        return arrived[: len(others)]

    def tie(value, sums):
        value, held_sums = lax.optimization_barrier((value, [one.value for one in sums]))
        for one, held_sum in zip(sums, held_sums):
            one.value = held_sum
        return value

    x_mask = geo.x_last[-2]
    quarter = D // 4
    quarters = [turn_x[:, k * quarter : (k + 1) * quarter] for k in range(4)]

    def four_rows(values, quarters):
        tall = jnp.concatenate(values, axis=0)
        stay, to_x, to_core, to_both = (mm(tall, q).astype(BF16) for q in quarters)
        size = tall.shape[0]
        from_x = sw(jnp.concatenate([to_x, to_both], axis=0), x_mask)
        rest = sw(jnp.concatenate([to_core, from_x[size:]], axis=0), core)
        spots = [slice(k * tokens, (k + 1) * tokens) for k in range(len(values))]
        return [
            jnp.concatenate([stay[s], from_x[:size][s], rest[:size][s], rest[size:][s]], axis=0) for s in spots
        ]

    def two_tokens(value):
        return jnp.concatenate([value, sw(value, x_mask)], axis=0)

    def four_tokens(value):
        return jnp.concatenate([value, sw(value, core)], axis=0)

    def side_by_side(parts):
        return jnp.concatenate([part.astype(BF16) for part in parts], axis=1)

    def fold(value, a):
        return tuple(side[a * tokens : (a + 1) * tokens] for side in value)

    def half_moves(parity):
        moves = []
        for b in range(geo.b):
            for block in range(n):
                h = 2 * block + parity
                to = geo.device(b, h if h < n else 2 * n - 1 - h)
                moves.append((b * n + block, to))
        return moves

    near_masks = list(geo.plane)
    masks = [geo.rank_mask(m) for m in near_masks] + [geo.rank_mask(m ^ core) for m in near_masks]
    if len(near_masks) == 4:
        near_sources = [(k, part * half, m, part) for k, m in enumerate(masks[:3]) for part in range(2)]
        near_sources += [(3, 0, masks[3], 0), (4, 0, masks[3], 1)]
    else:
        near_sources = [(k, part * half, m, part) for k, m in enumerate(masks[:n // 2]) for part in range(2)]
    piece_count = near_sources[-1][0] + 1
    sources = near_sources + [
        (k + piece_count, row, m ^ geo.rank_mask(core), part) for k, row, m, part in near_sources
    ]

    spread_pre = [jnp.repeat(mix_pre[l].T, E, axis=1) * E ** (-0.5) for l in range(LAYERS)]
    spread_post = [jnp.repeat(mix_post[l], E, axis=1) for l in range(LAYERS)]

    def spread_keys(own):
        if len(near_masks) == 4:
            y, x = near_masks[1], near_masks[2]
            by_y, by_x = sw(own, y), sw(own, x)
            return [own, by_y, by_x, sw(by_x[:half], y), sw(by_y[half:], x)]
        return [own] + [sw(own, m) for m in near_masks[1:]]

    saved = []
    for l in range(LAYERS):
        gain_a, gain_f = gain_all[2 * l], gain_all[2 * l + 1]
        turn = turns[l]
        n1 = (stream * norm_parts(stream) * gain_a).astype(BF16)
        projected = times(relative(n1, turn), attns[l], 0, 3 * D).astype(BF16)
        queries = projected[:, :D]
        if timed and l == 0:
            end_round(fifth, projected)
            sixth = begin_round(5, projected)
        pieces = spread_keys(projected[:, D:])
        pieces = pieces + [sw(piece, core) for piece in pieces]
        attended, lse, pv = attend(n, sources, rank_arg, queries, pieces, spread_pre[l], spread_post[l])
        if timed:
            end_round(sixth if l == 0 else eighth, attended)
        if l == 0:
            if timed:
                seventh = begin_round(6, attended)
            outwards[0], attns[1] = finish(1)
        else:
            inwards[1], outwards[1] = finish(2)
        middle = stream + times(relative(attended, turn), attns[l], 3 * D, D)
        n2 = (middle * norm_parts(middle) * gain_f).astype(BF16)
        hidden = times(relative(n2, turns[1 - l]), inwards[l], 0, ff)
        active = jax.nn.gelu(hidden, approximate=True).astype(BF16)
        wide = relative(jnp.concatenate([active[:, a * D : (a + 1) * D] for a in range(folds)], axis=0), turns[l])
        stream_in, stream = stream, middle
        for a in range(folds):
            stream = stream + times(fold(wide, a), outwards[l], a * D, D)
        if timed and l == 0:
            end_round(seventh, stream)
            eighth = begin_round(7, stream)
        saved.append((stream_in, n1, queries, pieces, attended, lse, pv, middle, n2, hidden, active, wide))

    flat, _ = lax.optimization_barrier((cotangent.reshape(tokens, D), saved[1][0]))
    evens = lax.ppermute(flat[:half], AXES, half_moves(0))
    odds = lax.ppermute(flat[half:], AXES, half_moves(1))
    even_rank = rank % 2 == 0
    grad_stream = jnp.where(
        even_rank, jnp.concatenate([evens, odds], axis=0), jnp.concatenate([odds, evens], axis=0)
    ).astype(F32)

    final = stream.astype(BF16)
    back_even = [(b, a) for a, b in half_moves(0)]
    back_odd = [(b, a) for a, b in half_moves(1)]
    first = jnp.where(even_rank, final[:half], final[half:])
    second = jnp.where(even_rank, final[half:], final[:half])
    output = [lax.ppermute(first, AXES, back_even), lax.ppermute(second, AXES, back_odd)]

    mixes = [None] * LAYERS
    gain_grads = [None] * LAYERS
    for l in reversed(range(LAYERS)):
        gain_a, gain_f = gain_all[2 * l], gain_all[2 * l + 1]
        stream_in, n1, queries, pieces, attended, lse, pv, middle, n2, hidden, active, wide = saved[l]
        gf = grad_stream.astype(BF16)
        pull = jax.vjp(lambda z: jax.nn.gelu(z, approximate=True), hidden)[1]
        active_grad = [back_times(gf, outwards[l], a * D, D, turns[l]) for a in range(folds)]
        gz = pull(jnp.concatenate(active_grad, axis=1))[0].astype(BF16)
        normed_grad = back_times(gz, inwards[l], 0, ff, turns[1 - l])
        by_fold = [active[:, a * D : (a + 1) * D] for a in range(folds)]
        gf_two = two_tokens(gf)
        if l == 0:
            tall = four_rows(by_fold, quarters)
            tall_n2, tall_out, tall_n1 = four_rows([n2, attended, n1], quarters)
        else:
            gz_two = two_tokens(gz)
            tall = four_rows([n2] + by_fold, quarters)
        delta, gain_f_grad = norm_back(middle, gain_f, normed_grad)
        middle_grad = grad_stream + delta
        gy = middle_grad.astype(BF16)
        go = back_times(gy, attns[l], 3 * D, D, turns[l]).astype(BF16)
        if l == 0:
            gz_two = two_tokens(jnp.concatenate([gz, gy], axis=1))
            go, gf_two = lax.optimization_barrier((go, gf_two))
            gf_four = four_tokens(gf_two)
            back_sum = Sum(side_by_side([t_mm(part, gf_four) for part in tall]), geo.x_last)
            back_sum.step()
            ffn_sum.step()
        gq, pre_grad, post_grad, parts = attend_back(
            sources, masks, rank_arg, queries, go, lse, pv, pieces, spread_pre[l], spread_post[l]
        )
        mixes[l] = (pre_grad, post_grad)
        if l == 1:
            parts, output = lax.optimization_barrier((parts, output))
        if l == 0:
            parts, gz_two, both_two = lax.optimization_barrier((parts, gz_two, both_two))
            parts = tie(parts, [back_sum, ffn_sum])
        size = len(near_masks)
        sums = [parts[k].astype(F32) + sw(parts[size + k], core).astype(F32) for k in range(size)]
        others = [(sums[k].astype(BF16), near_masks[k]) for k in range(1, size)]
        if l == 0:
            arrived = exchange(parts[0], [ffn_sum], others)
            gz_two, both_two, _ = lax.optimization_barrier((gz_two, both_two, sums))
            gz_four, both = four_tokens(gz_two), four_tokens(both_two)
            attn_grad = [t_mm(tall_n1_one, both[:, : 3 * D]), t_mm(tall_out_one, both[:, 3 * D :])]
            in_grad = [t_mm(tall_n2, gz_four[:, :ff]), t_mm(tall_out, gz_four[:, ff:])]
            joined_sum = Sum(side_by_side(attn_grad + in_grad), geo.x_last)
            arrived = tie(arrived, [joined_sum])
        else:
            arrived = [sw(value, mask) for value, mask in others]
            gz_two, gf_two, _ = lax.optimization_barrier((gz_two, gf_two, sums))
            gz_four, gf_four = four_tokens(gz_two), four_tokens(gf_two)
            ffn_grad = [t_mm(tall[0], gz_four)] + [t_mm(part, gf_four) for part in tall[1:]]
            ffn_sum = Sum(side_by_side(ffn_grad), geo.x_last)
            arrived = tie(arrived, [ffn_sum])
        kv_grad = sums[0]
        for there in arrived:
            kv_grad = kv_grad + there.astype(F32)
        joint = jnp.concatenate([gq, kv_grad.astype(BF16)], axis=1)
        normed_grad = back_times(joint, attns[l], 0, 3 * D, turns[l])
        if l == 0:
            joint_zero = joint
        else:
            both_two = two_tokens(jnp.concatenate([joint, gy], axis=1))
            tall_n1_one, tall_out_one = four_rows([n1, attended], quarters)
        delta, gain_a_grad = norm_back(stream_in, gain_a, normed_grad)
        grad_stream = middle_grad + delta
        gain_grads[l] = (gain_a_grad, gain_f_grad)

    pre_sum = jnp.stack([mixes[l][0] for l in range(LAYERS)]).reshape(LAYERS, H, H, E).sum(-1)
    post_sum = jnp.stack([mixes[l][1] for l in range(LAYERS)]).reshape(LAYERS, H, H, E).sum(-1)
    small = jnp.concatenate(
        [(pre_sum.transpose(0, 2, 1) * E ** (-0.5)).reshape(-1), post_sum.reshape(-1)]
        + [gain_grads[l][k] for k in range(2) for l in range(LAYERS)]
    )
    size = small.shape[0]
    small = jnp.pad(small, (0, -size % 1024)).reshape(-1, 128)
    small_masks = bits(1, count)

    g0 = grad_stream.astype(BF16)
    arrived = exchange(g0, [joined_sum], [(joint_zero, x_mask)] + [(g0, m) for m in geo.zs[1:]])
    joint_four = four_tokens(jnp.concatenate([joint_zero, arrived[0]], axis=0))
    qkv_sum = Sum(t_mm(tall_n1, joint_four).astype(BF16), geo.x_last)
    rows = jnp.concatenate([g0] + arrived[1:], axis=0)

    def share_small(after, sums, others=()):
        nonlocal small
        there = exchange(after, sums, list(others) + [(small, small_masks.pop())])
        small = small + there[-1]
        return there[:-1]

    if len(geo.plane) == 4:
        cut = rows.shape[0] // 2
        y, x = geo.plane[1], geo.plane[2]
        by_y, by_x = share_small(rows, [joined_sum, back_sum], [(rows, y), (rows, x)])
        both = share_small(by_x, [qkv_sum, joined_sum], [(by_x[:cut], y), (by_y[cut:], x)])
        blocks = [rows, by_y, by_x] + both
    else:
        blocks = [rows] + share_small(rows, [joined_sum, back_sum], [(rows, m) for m in geo.plane[1:]])
        share_small(blocks[-1], [qkv_sum, joined_sum])
    blocks = blocks + [sw(block, core) for block in blocks]
    share_small(blocks, [qkv_sum, back_sum, ffn_sum])
    own_names = me * vocab + line
    blocks = jnp.concatenate(blocks, axis=0)
    embedding_grad = mm(
        (own_names[:, None] == ids[None, :]).astype(BF16), blocks
    )
    while len(small_masks) > 2:
        share_small(qkv_sum.value, [qkv_sum])
    one_bit, two_bit = small_masks
    one, two, both = exchange(qkv_sum.value, [qkv_sum], [(small, one_bit), (small, two_bit), (small, one_bit ^ two_bit)])
    small = (small + one) + (two + both)
    small = small.reshape(-1)[:size]
    mix = small[: 2 * LAYERS * H * H].reshape(2, LAYERS, H, H)
    gain_sum = small[2 * LAYERS * H * H :].reshape(2, LAYERS, D)
    gain_sum = lax.dynamic_slice(gain_sum, (0, 0, me * share), (2, LAYERS, share))

    def in_order(part):
        return part.reshape(share, folds, count, share).transpose(0, 2, 1, 3).reshape(share, ff)

    def back_order(part):
        return jnp.concatenate([part[:, a * D : (a + 1) * D] for a in range(folds)], axis=0)

    qkv_share = qkv_sum.result()
    one, joined, zero = ffn_sum.result(), joined_sum.result(), back_sum.result()
    attn_share, in_share = joined[:, : 4 * D], joined[:, 4 * D :]
    output = jnp.concatenate(output, axis=0).reshape(cotangent.shape)
    return (
        output,
        embedding_grad,
        gain_sum[0],
        jnp.stack([qkv_share, attn_share[:, : 3 * D]]),
        jnp.stack([in_share[:, ff:], attn_share[:, 3 * D :]]),
        gain_sum[1],
        jnp.stack([in_order(in_share[:, :ff]), in_order(one[:, :ff])]),
        jnp.stack([back_order(zero), back_order(one[:, ff:])]),
        mix[0],
        mix[1],
    )


def solution(mesh):
    everywhere = ("batch", "seq")
    weight = P(None, everywhere, None)
    vector = P(None, everywhere)
    return jax.shard_map(
        functools.partial(shards, Geometry(mesh)),
        mesh=mesh,
        in_specs=(
            P("batch", "seq"),
            P(everywhere, None),
            vector,
            weight,
            weight,
            vector,
            weight,
            weight,
            P(),
            P(),
            P("batch", "seq", None),
        ),
        out_specs=(
            P("batch", "seq", None),
            P(everywhere, None),
            vector,
            weight,
            weight,
            vector,
            weight,
            weight,
            P(),
            P(),
        ),
        check_vma=False,
    )
```

```python
import functools

import jax
import jax.numpy as jnp
from jax import lax
from jax.experimental import pallas as pl
from jax.experimental.pallas import tpu as pltpu
from jax.sharding import PartitionSpec as P

D = 768
H = 12
E = 64
LAYERS = 2
AXES = ("batch", "seq")
NEGATIVE = -1e30
CHUNK = 256
F32 = jnp.float32
BF16 = jnp.bfloat16


class Geometry:
    def __init__(self, mesh):
        self.b = mesh.shape["batch"]
        self.n = mesh.shape["seq"]
        self.r = self.n // self.b
        self.count = self.b * self.n
        self.core = self.n
        low = list(range(self.r))
        self.high = [k * self.n for k in range(0, self.b, 2)]
        self.low = low
        self.plane = [h + l for h in self.high for l in low]
        self.zs = [k * self.r for k in range(self.b)]
        self.order = [c + h + l + z for c in (0, self.core) for h in self.high for l in low for z in self.zs]
        z_bits = bits(self.r, self.n)[::-1]
        x_bits = [bit for bit in bits(self.n, self.count) if bit != self.core]
        y_bits = bits(1, self.r)
        self.x_last = z_bits + y_bits + x_bits + [self.core]
        self.y_last = z_bits + x_bits + y_bits + [self.core]

    def rank_mask(self, mask):
        return (mask // self.n) * self.r + mask % self.n

    def device(self, sequence, rank):
        return (rank // self.r) * self.n + sequence * self.r + rank % self.r


def bits(first, end):
    found = []
    while first < end:
        found.append(first)
        first *= 2
    return found


def reached(masks):
    order = [0]
    for mask in masks:
        order = order + [o ^ mask for o in order]
    return order


def swap(value, mask, count):
    return lax.ppermute(value, AXES, [(p, p ^ mask) for p in range(count)])


def dot(a, b, contract):
    return lax.dot_general(a, b, (contract, ((), ())), preferred_element_type=F32)


def load_keys(sources, n, half, rank, pieces, kv, sems):
    copies = []
    for k, (index, row, mask, part) in enumerate(sources):
        owner = rank ^ mask
        place = owner if part == 0 else 2 * n - 1 - owner
        copies.append(
            pltpu.make_async_copy(
                pieces[index].at[pl.ds(row, half)],
                kv.at[pl.ds(pl.multiple_of(place * half, half), half)],
                sems.at[k],
            )
        )
    for copy in copies:
        copy.start()
    return copies


def mixed_rows(rows, weights):
    return jnp.concatenate([rows * weights[g : g + 1, :] for g in range(H)], axis=0)


def forward_kernel(n, sources, count, half, rank_ref, q_ref, pre_ref, post_ref, *rest):
    pieces = rest[:count]
    o_ref, lse_ref, pv_ref = rest[count : count + 3]
    kv, qg, logits, top, total, acc, sems = rest[count + 3 :]
    rank = rank_ref[0]
    rows = H * half
    copies = load_keys(sources, n, half, rank, pieces, kv, sems)
    for copy in copies:
        copy.wait()
    for part in range(2):
        place = rank if part == 0 else 2 * n - 1 - rank
        live = (place * half + half + CHUNK - 1) // CHUNK
        q_part = q_ref[part * half : (part + 1) * half, :].astype(F32)
        qg[...] = mixed_rows(q_part, pre_ref[...]).astype(BF16)
        top[...] = jnp.full((rows, 128), NEGATIVE, F32)
        total[...] = jnp.zeros((rows, 128), F32)
        acc[...] = jnp.zeros((rows, D), F32)
        spot = place * half + lax.broadcasted_iota(jnp.int32, (rows, CHUNK), 0) % half
        lane = lax.broadcasted_iota(jnp.int32, (rows, CHUNK), 1)

        def score(c, carry):
            start = pl.multiple_of(c * CHUNK, CHUNK)
            found = dot(qg[...], kv[pl.ds(start, CHUNK), :D], ((1,), (1,)))
            found = jnp.where(start + lane <= spot, found, NEGATIVE)
            logits[c] = found
            best = found[:, :128]
            for k in range(1, CHUNK // 128):
                best = jnp.maximum(best, found[:, k * 128 : (k + 1) * 128])
            top[...] = jnp.maximum(top[...], best)
            return carry

        lax.fori_loop(0, live, score, 0)
        row_max = jnp.max(top[...], axis=1, keepdims=True)

        def weigh(c, carry):
            start = pl.multiple_of(c * CHUNK, CHUNK)
            prob = jnp.exp(logits[c] - row_max)
            part_sum = prob[:, :128]
            for k in range(1, CHUNK // 128):
                part_sum = part_sum + prob[:, k * 128 : (k + 1) * 128]
            total[...] += part_sum
            acc[...] += dot(prob.astype(BF16), kv[pl.ds(start, CHUNK), D:], ((1,), (0,)))
            return carry

        lax.fori_loop(0, live, weigh, 0)
        row_sum = jnp.sum(total[...], axis=1, keepdims=True)
        scale = 1.0 / row_sum
        lse = jnp.broadcast_to(row_max + jnp.log(row_sum), (rows, 128))
        lse_ref[part] = jnp.transpose(lse)[:8, :]
        out = jnp.zeros((half, D), F32)
        for g in range(H):
            normal = acc[g * half : (g + 1) * half, :] * scale[g * half : (g + 1) * half, :]
            pv_ref[part, g * half : (g + 1) * half, :] = normal.astype(BF16)
            out = out + normal * post_ref[g : g + 1, :]
        o_ref[part * half : (part + 1) * half, :] = out.astype(BF16)


def backward_kernel(n, sources, count, masks, half, rank_ref, q_ref, go_ref, lse_ref, pv_ref, pre_ref, post_ref, *rest):
    pieces = rest[:count]
    gq_ref, pre_grad_ref, post_grad_ref = rest[count : count + 3]
    grads = rest[count + 3 : count + 3 + n]
    kv, qg, gg, gk, gv, acc, sems, out_sems = rest[count + 3 + n :]
    rank = rank_ref[0]
    rows = H * half
    copies = load_keys(sources, n, half, rank, pieces, kv, sems)
    gk[...] = jnp.zeros(gk.shape, F32)
    gv[...] = jnp.zeros(gv.shape, F32)
    pre_grad_ref[...] = jnp.zeros(pre_grad_ref.shape, F32)
    post_grad_ref[...] = jnp.zeros(post_grad_ref.shape, F32)
    for copy in copies:
        copy.wait()
    for part in range(2):
        place = rank if part == 0 else 2 * n - 1 - rank
        live = (place * half + half + CHUNK - 1) // CHUNK
        q_part = q_ref[part * half : (part + 1) * half, :].astype(F32)
        go_part = go_ref[part * half : (part + 1) * half, :].astype(F32)
        row_dots = []
        for g in range(H):
            qg[g * half : (g + 1) * half, :] = (q_part * pre_ref[g : g + 1, :]).astype(BF16)
            mixed = go_part * post_ref[g : g + 1, :]
            gg[g * half : (g + 1) * half, :] = mixed.astype(BF16)
            normal = pv_ref[part, g * half : (g + 1) * half, :].astype(F32)
            row_dots.append(jnp.sum(mixed * normal, axis=1, keepdims=True))
            post_grad_ref[g : g + 1, :] += jnp.sum(go_part * normal, axis=0, keepdims=True)
        row_dot = jnp.broadcast_to(jnp.concatenate(row_dots, axis=0), (rows, 128))
        row_dot = jnp.transpose(row_dot)[:1, :]
        lse = lse_ref[part][:1, :]
        acc[...] = jnp.zeros((rows, D), F32)
        spot = place * half + lax.broadcasted_iota(jnp.int32, (CHUNK, rows), 1) % half
        line = lax.broadcasted_iota(jnp.int32, (CHUNK, rows), 0)

        def block(c, carry):
            start = pl.multiple_of(c * CHUNK, CHUNK)
            keys = kv[pl.ds(start, CHUNK), :D]
            values = kv[pl.ds(start, CHUNK), D:]
            found = dot(keys, qg[...], ((1,), (1,)))
            found = jnp.where(start + line <= spot, found, NEGATIVE)
            prob = jnp.exp(found - lse)
            grad_prob = dot(values, gg[...], ((1,), (1,)))
            grad_logit = (prob * (grad_prob - row_dot)).astype(BF16)
            gv[pl.ds(start, CHUNK), :] += dot(prob.astype(BF16), gg[...], ((1,), (0,)))
            gk[pl.ds(start, CHUNK), :] += dot(grad_logit, qg[...], ((1,), (0,)))
            acc[...] += dot(grad_logit, keys, ((0,), (0,)))
            return carry

        lax.fori_loop(0, live, block, 0)
        gq = jnp.zeros((half, D), F32)
        for g in range(H):
            found = acc[g * half : (g + 1) * half, :]
            gq = gq + found * pre_ref[g : g + 1, :]
            pre_grad_ref[g : g + 1, :] += jnp.sum(found * q_part, axis=0, keepdims=True)
        gq_ref[part * half : (part + 1) * half, :] = gq.astype(BF16)
    kv[:, :D] = gk[...].astype(BF16)
    kv[:, D:] = gv[...].astype(BF16)
    copies = []
    for index, mask in enumerate(masks):
        owner = rank ^ mask
        for part, place in ((0, owner), (1, 2 * n - 1 - owner)):
            start = pl.multiple_of(place * half, half)
            copies.append(
                pltpu.make_async_copy(
                    kv.at[pl.ds(start, half)],
                    grads[index].at[pl.ds(part * half, half)],
                    out_sems.at[2 * index + part],
                )
            )
    for copy in copies:
        copy.start()
    for copy in copies:
        copy.wait()


VMEM = pl.BlockSpec(memory_space=pltpu.VMEM)
SMEM = pl.BlockSpec(memory_space=pltpu.SMEM)
ANY = pl.BlockSpec(memory_space=pl.ANY)
LIMIT = pltpu.CompilerParams(vmem_limit_bytes=58 * 2**20)


def attend(n, sources, rank, queries, pieces, pre, post):
    count = len(pieces)
    tokens = queries.shape[0]
    half = tokens // 2
    rows = H * half
    length = n * tokens
    return pl.pallas_call(
        functools.partial(forward_kernel, n, sources, count, half),
        out_shape=(
            jax.ShapeDtypeStruct((tokens, D), BF16),
            jax.ShapeDtypeStruct((2, 8, rows), F32),
            jax.ShapeDtypeStruct((2, rows, D), BF16),
        ),
        in_specs=[SMEM, VMEM, VMEM, VMEM] + [ANY] * count,
        out_specs=(VMEM, VMEM, VMEM),
        scratch_shapes=[
            pltpu.VMEM((length, 2 * D), BF16),
            pltpu.VMEM((rows, D), BF16),
            pltpu.VMEM((length // CHUNK, rows, CHUNK), F32),
            pltpu.VMEM((rows, 128), F32),
            pltpu.VMEM((rows, 128), F32),
            pltpu.VMEM((rows, D), F32),
            pltpu.SemaphoreType.DMA((2 * n,)),
        ],
        compiler_params=LIMIT,
        cost_estimate=pl.CostEstimate(flops=10**8, bytes_accessed=8 * 2**20, transcendentals=2**20),
        name="attend",
    )(rank, queries, pre, post, *pieces)


def attend_back(sources, masks, rank, queries, grad_out, lse, pv, pieces, pre, post):
    n = len(masks)
    count = len(pieces)
    tokens = queries.shape[0]
    half = tokens // 2
    rows = H * half
    length = n * tokens
    outs = pl.pallas_call(
        functools.partial(backward_kernel, n, sources, count, masks, half),
        out_shape=(
            jax.ShapeDtypeStruct((tokens, D), BF16),
            jax.ShapeDtypeStruct((H, D), F32),
            jax.ShapeDtypeStruct((H, D), F32),
        )
        + tuple(jax.ShapeDtypeStruct((tokens, 2 * D), BF16) for _ in masks),
        in_specs=[SMEM] + [VMEM] * 6 + [ANY] * count,
        out_specs=(VMEM, VMEM, VMEM) + (ANY,) * n,
        scratch_shapes=[
            pltpu.VMEM((length, 2 * D), BF16),
            pltpu.VMEM((rows, D), BF16),
            pltpu.VMEM((rows, D), BF16),
            pltpu.VMEM((length, D), F32),
            pltpu.VMEM((length, D), F32),
            pltpu.VMEM((rows, D), F32),
            pltpu.SemaphoreType.DMA((2 * n,)),
            pltpu.SemaphoreType.DMA((2 * n,)),
        ],
        compiler_params=LIMIT,
        cost_estimate=pl.CostEstimate(flops=16 * 10**9, bytes_accessed=12 * 2**20, transcendentals=2**20),
        name="attend_back",
    )(rank, queries, grad_out, lse, pv, pre, post, *pieces)
    return outs[0], outs[1], outs[2], outs[3:]


def mm(a, b):
    return jnp.dot(a, b, preferred_element_type=F32)


def mm_t(a, b):
    return lax.dot_general(a, b, (((1,), (1,)), ((), ())), preferred_element_type=F32)


def t_mm(a, b):
    return lax.dot_general(a, b, (((0,), (0,)), ((), ())), preferred_element_type=F32)


def norm_parts(x):
    return lax.rsqrt(jnp.mean(x * x, axis=-1, keepdims=True) + 1e-06)


def norm_back(x, gain, grad):
    r = norm_parts(x)
    gain_grad = jnp.sum(grad * x * r, axis=0)
    scaled = grad * gain
    x_grad = r * scaled - x * (r * r * r) * jnp.mean(scaled * x, axis=-1, keepdims=True)
    return x_grad, gain_grad


def shards(
    geo,
    token_ids,
    embedding,
    gain_attn,
    w_qkv,
    w_proj,
    gain_ffn,
    w_in,
    w_back,
    mix_pre,
    mix_post,
    cotangent,
):
    n, r, count, core = geo.n, geo.r, geo.count, geo.core
    tokens = token_ids.size
    half = tokens // 2
    i = lax.axis_index("batch")
    j = lax.axis_index("seq")
    me = i * n + j
    rank = i * r + j % r
    rank_arg = rank.reshape(1).astype(jnp.int32)
    share = w_qkv.shape[1]
    back_share = w_back.shape[1]
    folds = back_share // share
    ff = w_in.shape[2]
    sw = functools.partial(swap, count=count)

    def packed_in(l):
        return w_in[l].reshape(share, count, folds, share).transpose(0, 2, 1, 3).reshape(share, ff)

    def packed_back(l):
        return jnp.concatenate([w_back[l, a * share : (a + 1) * share] for a in range(folds)], axis=1)

    gains = jnp.stack([gain_attn[0], gain_ffn[0], gain_attn[1], gain_ffn[1]], axis=1)
    gains = jnp.pad(gains, ((0, 0), (0, 124)))
    wide = [w_qkv[0], w_proj[0], gains]
    pairs = [
        jnp.concatenate(wide + [packed_in(0), packed_back(0)][:1], axis=1),
        jnp.concatenate([packed_back(0), w_qkv[1], w_proj[1]], axis=1),
        jnp.concatenate([packed_in(1), packed_back(1)], axis=1),
    ]
    borders = [4 * D + gains.shape[1], folds * D, ff]
    routes = [geo.x_last, geo.y_last]
    shared = len(geo.zs).bit_length() - 1
    stages = len(geo.x_last) - 1
    timed = stages == 4
    split = [None] * len(pairs)
    last_round = [None]

    def begin_round(number, after, late=()):
        pending = []
        for p in range(len(pairs)):
            k = number - 2 * p
            if 0 <= k < shared:
                pending.append((p, None, geo.x_last[k], pairs[p]))
            elif shared <= k < stages:
                if k == shared:
                    split[p] = [pairs[p][:, : borders[p]], pairs[p][:, borders[p] :]]
                pending += [(p, side, routes[side][k], split[p][side]) for side in range(2)]
        values = [entry[3] for entry in pending]
        if timed:
            values = list(lax.optimization_barrier((values, after, last_round[0]))[0])
            for index, wait in late:
                values[index], _ = lax.optimization_barrier((values[index], wait))
        arrived = [sw(value, entry[2]) for value, entry in zip(values, pending)]
        last_round[0] = arrived
        return pending, values, arrived

    def end_round(state, hold):
        pending, values, arrived = state
        if timed and hold is not None:
            arrived = lax.optimization_barrier((arrived, hold))[0]
            last_round[0] = arrived
        for value, there, (p, side, _, _) in zip(values, arrived, pending):
            joined = jnp.concatenate([value, there], axis=0)
            if side is None:
                pairs[p] = joined
            else:
                split[p][side] = joined

    ids_route = [geo.x_last[-2]] + [m for m in geo.x_last[:-2]] + [core]
    ids = token_ids.reshape(1, tokens)
    ids_stages = []
    for mask in ids_route:
        ids = jnp.concatenate([ids, sw(ids, mask)], axis=0)
        ids_stages.append(ids)
    first_ids, deep_ids = ids_stages[0], ids_stages[len(geo.zs).bit_length() - 1]
    target = me ^ jnp.array(geo.order, jnp.int32)
    t_seq = (target % n) // r
    t_rank = (target // n) * r + target % r
    halves = jnp.stack([t_rank, 2 * n - 1 - t_rank], axis=1)
    source = (t_seq[:, None] * n + halves // 2) ^ me
    source = sum(((source // mask) % 2) * 2**k for k, mask in enumerate(ids_route))
    ids = jnp.take(ids.reshape(2 * count, half), (source * 2 + halves % 2).reshape(-1), axis=0).reshape(-1)

    vocab = embedding.shape[0]
    line = jnp.arange(vocab, dtype=jnp.int32)
    table, first_ids = lax.optimization_barrier((embedding, first_ids))
    tables = [table] + [sw(table, m) for m in geo.high[1:]]
    tables = tables + [sw(part, core) for part in tables]
    owners = geo.high + [m ^ core for m in geo.high]
    end_round(begin_round(0, deep_ids), None)
    end_round(begin_round(1, deep_ids), None)
    third = begin_round(2, deep_ids)
    near = ids[: len(geo.low) * len(geo.zs) * tokens]
    picked = jnp.zeros((near.shape[0], D), F32)
    for m, part in zip(owners, tables):
        picked = picked + mm((near[:, None] == ((me ^ m) * vocab + line)[None, :]).astype(BF16), part)
    picked = picked.astype(BF16)
    end_round(third, picked)
    flat = picked.reshape(len(geo.low), -1, D)
    row = flat[0]
    for k in range(1, len(geo.low)):
        row = row + sw(flat[k], geo.low[k])
    fourth = begin_round(3, picked, [(1, row), (2, row)])
    row = row.reshape(len(geo.zs), tokens, D)
    stream = row[0]
    for k in range(1, len(geo.zs)):
        stream = stream + sw(row[k], geo.zs[k])
    stream = stream.astype(F32)
    end_round(fourth, stream)
    fifth = begin_round(4, stream)
    if not timed:
        end_round(fifth, None)
        for number in range(5, stages + 2 * len(pairs) - 2):
            end_round(begin_round(number, None), None)

    side = D // 2
    feature = jnp.arange(D, dtype=jnp.int32)

    def turner(route):
        order = jnp.repeat(jnp.array(reached(route), jnp.int32), share)
        origin = (me ^ order) * share + feature % share
        return (feature[:, None] == origin[None, :]).astype(BF16)

    turn_x, turn_y = turner(geo.x_last), turner(geo.y_last)

    def relative(value, turn):
        turned = mm(value, turn).astype(BF16)
        return turned[:, :side], turned[:, side:]

    def times(value, pair, start, width):
        near, far = pair
        return mm(value[0], near[:, start : start + width]) + mm(value[1], far[:, start : start + width])

    def back_times(value, pair, start, width, turn):
        near, far = pair
        near, far = (mm_t(value, side[:, start : start + width]).astype(BF16) for side in (near, far))
        return mm_t(jnp.concatenate([near, far], axis=1), turn)

    def finish(p):
        return [(value, sw(value, core)) for value in split[p]]

    turns = [turn_x, turn_y]
    attns, inwards, outwards = [None] * LAYERS, [None] * LAYERS, [None] * LAYERS
    attns[0], inwards[0] = finish(0)
    gain_all = jnp.concatenate([side[:, 4 * D : 4 * D + 8] for side in attns[0]], axis=0)
    gain_all = mm(turn_x, gain_all).T

    class Sum:
        def __init__(self, value, route):
            self.value = value
            self.masks = list(route[:-2])

        def outgoing(self):
            if not self.masks:
                return []
            return [(self.value[self.value.shape[0] // 2 :], self.masks.pop())]

        def incoming(self, arrived):
            for there in arrived:
                rows = self.value.shape[0] // 2
                self.value = self.value[:rows].astype(F32) + there.astype(F32)
                if self.masks:
                    self.value = self.value.astype(BF16)

        def step(self):
            self.incoming([sw(value, mask) for value, mask in self.outgoing()])

        def result(self):
            while self.masks:
                self.step()
            return self.value

    def exchange(after, sums, others=()):
        entries = list(others)
        spans = []
        for one in sums:
            out = one.outgoing()
            spans.append(len(out))
            entries += out
        values = lax.optimization_barrier(([value for value, _ in entries], after))[0]
        arrived = [sw(value, mask) for value, (_, mask) in zip(values, entries)]
        arrived = list(lax.optimization_barrier(arrived))
        place = len(others)
        for one, span in zip(sums, spans):
            one.incoming(arrived[place : place + span])
            place += span
        return arrived[: len(others)]

    def tie(value, sums):
        value, held_sums = lax.optimization_barrier((value, [one.value for one in sums]))
        for one, held_sum in zip(sums, held_sums):
            one.value = held_sum
        return value

    x_mask = geo.x_last[-2]
    quarter = D // 4
    quarters = [turn_x[:, k * quarter : (k + 1) * quarter] for k in range(4)]

    def four_rows(values, quarters):
        tall = jnp.concatenate(values, axis=0)
        stay, to_x, to_core, to_both = (mm(tall, q).astype(BF16) for q in quarters)
        size = tall.shape[0]
        from_x = sw(jnp.concatenate([to_x, to_both], axis=0), x_mask)
        rest = sw(jnp.concatenate([to_core, from_x[size:]], axis=0), core)
        spots = [slice(k * tokens, (k + 1) * tokens) for k in range(len(values))]
        return [
            jnp.concatenate([stay[s], from_x[:size][s], rest[:size][s], rest[size:][s]], axis=0) for s in spots
        ]

    def two_tokens(value):
        return jnp.concatenate([value, sw(value, x_mask)], axis=0)

    def four_tokens(value):
        return jnp.concatenate([value, sw(value, core)], axis=0)

    def side_by_side(parts):
        return jnp.concatenate([part.astype(BF16) for part in parts], axis=1)

    def fold(value, a):
        return tuple(side[a * tokens : (a + 1) * tokens] for side in value)

    def half_moves(parity):
        moves = []
        for b in range(geo.b):
            for block in range(n):
                h = 2 * block + parity
                to = geo.device(b, h if h < n else 2 * n - 1 - h)
                moves.append((b * n + block, to))
        return moves

    near_masks = list(geo.plane)
    masks = [geo.rank_mask(m) for m in near_masks] + [geo.rank_mask(m ^ core) for m in near_masks]
    if len(near_masks) == 4:
        near_sources = [(k, part * half, m, part) for k, m in enumerate(masks[:3]) for part in range(2)]
        near_sources += [(3, 0, masks[3], 0), (4, 0, masks[3], 1)]
    else:
        near_sources = [(k, part * half, m, part) for k, m in enumerate(masks[:n // 2]) for part in range(2)]
    piece_count = near_sources[-1][0] + 1
    sources = near_sources + [
        (k + piece_count, row, m ^ geo.rank_mask(core), part) for k, row, m, part in near_sources
    ]

    spread_pre = [jnp.repeat(mix_pre[l].T, E, axis=1) * E ** (-0.5) for l in range(LAYERS)]
    spread_post = [jnp.repeat(mix_post[l], E, axis=1) for l in range(LAYERS)]

    def spread_keys(own):
        if len(near_masks) == 4:
            y, x = near_masks[1], near_masks[2]
            by_y, by_x = sw(own, y), sw(own, x)
            return [own, by_y, by_x, sw(by_x[:half], y), sw(by_y[half:], x)]
        return [own] + [sw(own, m) for m in near_masks[1:]]

    saved = []
    for l in range(LAYERS):
        gain_a, gain_f = gain_all[2 * l], gain_all[2 * l + 1]
        turn = turns[l]
        n1 = (stream * norm_parts(stream) * gain_a).astype(BF16)
        projected = times(relative(n1, turn), attns[l], 0, 3 * D).astype(BF16)
        queries = projected[:, :D]
        if timed and l == 0:
            end_round(fifth, projected)
            sixth = begin_round(5, projected)
        pieces = spread_keys(projected[:, D:])
        pieces = pieces + [sw(piece, core) for piece in pieces]
        attended, lse, pv = attend(n, sources, rank_arg, queries, pieces, spread_pre[l], spread_post[l])
        if timed:
            end_round(sixth if l == 0 else eighth, attended)
        if l == 0:
            if timed:
                seventh = begin_round(6, attended)
            outwards[0], attns[1] = finish(1)
        else:
            inwards[1], outwards[1] = finish(2)
        middle = stream + times(relative(attended, turn), attns[l], 3 * D, D)
        n2 = (middle * norm_parts(middle) * gain_f).astype(BF16)
        hidden = times(relative(n2, turns[1 - l]), inwards[l], 0, ff)
        active = jax.nn.gelu(hidden, approximate=True).astype(BF16)
        wide = relative(jnp.concatenate([active[:, a * D : (a + 1) * D] for a in range(folds)], axis=0), turns[l])
        stream_in, stream = stream, middle
        for a in range(folds):
            stream = stream + times(fold(wide, a), outwards[l], a * D, D)
        if timed and l == 0:
            end_round(seventh, stream)
            eighth = begin_round(7, stream)
        saved.append((stream_in, n1, queries, pieces, attended, lse, pv, middle, n2, hidden, active, wide))

    flat, _ = lax.optimization_barrier((cotangent.reshape(tokens, D), saved[1][2]))
    evens = lax.ppermute(flat[:half], AXES, half_moves(0))
    odds = lax.ppermute(flat[half:], AXES, half_moves(1))
    even_rank = rank % 2 == 0
    grad_stream = jnp.where(
        even_rank, jnp.concatenate([evens, odds], axis=0), jnp.concatenate([odds, evens], axis=0)
    ).astype(F32)

    final = stream.astype(BF16)
    back_even = [(b, a) for a, b in half_moves(0)]
    back_odd = [(b, a) for a, b in half_moves(1)]
    first = jnp.where(even_rank, final[:half], final[half:])
    second = jnp.where(even_rank, final[half:], final[:half])
    output = [lax.ppermute(first, AXES, back_even), lax.ppermute(second, AXES, back_odd)]

    mixes = [None] * LAYERS
    gain_grads = [None] * LAYERS
    for l in reversed(range(LAYERS)):
        gain_a, gain_f = gain_all[2 * l], gain_all[2 * l + 1]
        stream_in, n1, queries, pieces, attended, lse, pv, middle, n2, hidden, active, wide = saved[l]
        gf = grad_stream.astype(BF16)
        pull = jax.vjp(lambda z: jax.nn.gelu(z, approximate=True), hidden)[1]
        active_grad = [back_times(gf, outwards[l], a * D, D, turns[l]) for a in range(folds)]
        gz = pull(jnp.concatenate(active_grad, axis=1))[0].astype(BF16)
        normed_grad = back_times(gz, inwards[l], 0, ff, turns[1 - l])
        by_fold = [active[:, a * D : (a + 1) * D] for a in range(folds)]
        gf_two = two_tokens(gf)
        if l == 0:
            tall = four_rows(by_fold, quarters)
            tall_n2, tall_out, tall_n1 = four_rows([n2, attended, n1], quarters)
        else:
            gz_two = two_tokens(gz)
            tall = four_rows([n2] + by_fold, quarters)
        delta, gain_f_grad = norm_back(middle, gain_f, normed_grad)
        middle_grad = grad_stream + delta
        gy = middle_grad.astype(BF16)
        go = back_times(gy, attns[l], 3 * D, D, turns[l]).astype(BF16)
        if l == 0:
            gz_two = two_tokens(jnp.concatenate([gz, gy], axis=1))
            go, gf_two = lax.optimization_barrier((go, gf_two))
            gf_four = four_tokens(gf_two)
            back_sum = Sum(side_by_side([t_mm(part, gf_four) for part in tall]), geo.x_last)
            back_sum.step()
            ffn_sum.step()
        gq, pre_grad, post_grad, parts = attend_back(
            sources, masks, rank_arg, queries, go, lse, pv, pieces, spread_pre[l], spread_post[l]
        )
        mixes[l] = (pre_grad, post_grad)
        if l == 1:
            parts, output = lax.optimization_barrier((parts, output))
        if l == 0:
            parts, gz_two, both_two = lax.optimization_barrier((parts, gz_two, both_two))
            parts = tie(parts, [back_sum, ffn_sum])
        size = len(near_masks)
        sums = [parts[k].astype(F32) + sw(parts[size + k], core).astype(F32) for k in range(size)]
        others = [(sums[k].astype(BF16), near_masks[k]) for k in range(1, size)]
        if l == 0:
            arrived = exchange(parts[0], [ffn_sum], others)
            gz_two, both_two, _ = lax.optimization_barrier((gz_two, both_two, sums))
            gz_four, both = four_tokens(gz_two), four_tokens(both_two)
            attn_grad = [t_mm(tall_n1_one, both[:, : 3 * D]), t_mm(tall_out_one, both[:, 3 * D :])]
            in_grad = [t_mm(tall_n2, gz_four[:, :ff]), t_mm(tall_out, gz_four[:, ff:])]
            joined_sum = Sum(side_by_side(attn_grad + in_grad), geo.x_last)
            arrived = tie(arrived, [joined_sum])
        else:
            arrived = [sw(value, mask) for value, mask in others]
            gz_two, gf_two, _ = lax.optimization_barrier((gz_two, gf_two, sums))
            gz_four, gf_four = four_tokens(gz_two), four_tokens(gf_two)
            ffn_grad = [t_mm(tall[0], gz_four)] + [t_mm(part, gf_four) for part in tall[1:]]
            ffn_sum = Sum(side_by_side(ffn_grad), geo.x_last)
            arrived = tie(arrived, [ffn_sum])
        kv_grad = sums[0]
        for there in arrived:
            kv_grad = kv_grad + there.astype(F32)
        joint = jnp.concatenate([gq, kv_grad.astype(BF16)], axis=1)
        normed_grad = back_times(joint, attns[l], 0, 3 * D, turns[l])
        if l == 0:
            joint_zero = joint
        else:
            both_two = two_tokens(jnp.concatenate([joint, gy], axis=1))
            tall_n1_one, tall_out_one = four_rows([n1, attended], quarters)
        delta, gain_a_grad = norm_back(stream_in, gain_a, normed_grad)
        grad_stream = middle_grad + delta
        gain_grads[l] = (gain_a_grad, gain_f_grad)

    pre_sum = jnp.stack([mixes[l][0] for l in range(LAYERS)]).reshape(LAYERS, H, H, E).sum(-1)
    post_sum = jnp.stack([mixes[l][1] for l in range(LAYERS)]).reshape(LAYERS, H, H, E).sum(-1)
    small = jnp.concatenate(
        [(pre_sum.transpose(0, 2, 1) * E ** (-0.5)).reshape(-1), post_sum.reshape(-1)]
        + [gain_grads[l][k] for k in range(2) for l in range(LAYERS)]
    )
    size = small.shape[0]
    small = jnp.pad(small, (0, -size % 1024)).reshape(-1, 128)
    small_masks = bits(1, count)

    g0 = grad_stream.astype(BF16)
    arrived = exchange(g0, [joined_sum], [(joint_zero, x_mask)] + [(g0, m) for m in geo.zs[1:]])
    joint_four = four_tokens(jnp.concatenate([joint_zero, arrived[0]], axis=0))
    qkv_sum = Sum(t_mm(tall_n1, joint_four).astype(BF16), geo.x_last)
    rows = jnp.concatenate([g0] + arrived[1:], axis=0)

    def share_small(after, sums, others=()):
        nonlocal small
        there = exchange(after, sums, list(others) + [(small, small_masks.pop())])
        small = small + there[-1]
        return there[:-1]

    if len(geo.plane) == 4:
        cut = rows.shape[0] // 2
        y, x = geo.plane[1], geo.plane[2]
        by_y, by_x = share_small(rows, [joined_sum, back_sum], [(rows, y), (rows, x)])
        both = share_small(by_x, [qkv_sum, joined_sum], [(by_x[:cut], y), (by_y[cut:], x)])
        blocks = [rows, by_y, by_x] + both
    else:
        blocks = [rows] + share_small(rows, [joined_sum, back_sum], [(rows, m) for m in geo.plane[1:]])
        share_small(blocks[-1], [qkv_sum, joined_sum])
    blocks = blocks + [sw(block, core) for block in blocks]
    share_small(blocks, [qkv_sum, back_sum, ffn_sum])
    own_names = me * vocab + line
    blocks = jnp.concatenate(blocks, axis=0)
    embedding_grad = mm(
        (own_names[:, None] == ids[None, :]).astype(BF16), blocks
    )
    while len(small_masks) > 2:
        share_small(qkv_sum.value, [qkv_sum])
    one_bit, two_bit = small_masks
    one, two, both = exchange(qkv_sum.value, [qkv_sum], [(small, one_bit), (small, two_bit), (small, one_bit ^ two_bit)])
    small = (small + one) + (two + both)
    small = small.reshape(-1)[:size]
    mix = small[: 2 * LAYERS * H * H].reshape(2, LAYERS, H, H)
    gain_sum = small[2 * LAYERS * H * H :].reshape(2, LAYERS, D)
    gain_sum = lax.dynamic_slice(gain_sum, (0, 0, me * share), (2, LAYERS, share))

    def in_order(part):
        return part.reshape(share, folds, count, share).transpose(0, 2, 1, 3).reshape(share, ff)

    def back_order(part):
        return jnp.concatenate([part[:, a * D : (a + 1) * D] for a in range(folds)], axis=0)

    qkv_share = qkv_sum.result()
    one, joined, zero = ffn_sum.result(), joined_sum.result(), back_sum.result()
    attn_share, in_share = joined[:, : 4 * D], joined[:, 4 * D :]
    output = jnp.concatenate(output, axis=0).reshape(cotangent.shape)
    return (
        output,
        embedding_grad,
        gain_sum[0],
        jnp.stack([qkv_share, attn_share[:, : 3 * D]]),
        jnp.stack([in_share[:, ff:], attn_share[:, 3 * D :]]),
        gain_sum[1],
        jnp.stack([in_order(in_share[:, :ff]), in_order(one[:, :ff])]),
        jnp.stack([back_order(zero), back_order(one[:, ff:])]),
        mix[0],
        mix[1],
    )


def solution(mesh):
    everywhere = ("batch", "seq")
    weight = P(None, everywhere, None)
    vector = P(None, everywhere)
    return jax.shard_map(
        functools.partial(shards, Geometry(mesh)),
        mesh=mesh,
        in_specs=(
            P("batch", "seq"),
            P(everywhere, None),
            vector,
            weight,
            weight,
            vector,
            weight,
            weight,
            P(),
            P(),
            P("batch", "seq", None),
        ),
        out_specs=(
            P("batch", "seq", None),
            P(everywhere, None),
            vector,
            weight,
            weight,
            vector,
            weight,
            weight,
            P(),
            P(),
        ),
        check_vma=False,
    )
```
